128 devices in a mesh: lat: 2 (over z_lo), lon: 32 (over y, x, z_hi), tp: 2 (over core).
Axes of the slice: x: 4, y: 4, z: 4 (z_hi: 2, z_lo: 2; z = z_hi * 2 + z_lo), core: 2. Of those that a mesh axis runs over, the one named last changes fastest.
Arguments:
- tokens: bfloat16 [48, 768, 2, 1024], P('lat', 'lon', 'tp'), may hold values from -6 to 6
- land_mask: int32 [48, 768, 2], P('lat', 'lon', 'tp'), may hold values 0 or 1
- qkv_weight: bfloat16 [3, 1024, 1024], P(None, None, 'tp'), may hold values from -0.1875 to 0.1875
- out_weight: bfloat16 [1024, 1024], P('tp'), may hold values from -0.1875 to 0.1875
- out_grad: bfloat16 [48, 768, 2, 1024], P('lat', 'lon', 'tp'), may hold values from -6 to 6
Outputs:
- d_tokens: bfloat16 [48, 768, 2, 1024], P('lat', 'lon', 'tp')
- d_qkv_weight: float32 [3, 1024, 1024], P(None, 'lon', 'tp')
- d_out_weight: float32 [1024, 1024], P('tp', 'lon')
The draws below stay inside these ranges and needn't reach their ends.
All inputs are finite; a program needn't handle non-finite values. No bound on the sum of `land_mask` on one device may be relied on, other than what follows from the above.
Results may differ from the reference program's by a relative error of at most 0.03.
The reference program's roundings to bfloat16 on the way count: a program that leaves them out, or rounds other values in their place, can miss the bound.
Values may be sent and summed in bfloat16 or wider, within the bound.
A program may use at most 128 MiB of HBM per device.

```python
import jax
import jax.numpy as jnp
from jax import lax

D = 1024
HEAD_DIM = 64
LEV = 2
WIN_LAT = 6
WIN_LON = 12
SHIFT_LAT = 3
SHIFT_LON = 6
NLAT = 48
NLON = 768


def draw_qkv_weight(key, part):
    key = jax.random.fold_in(key, 11)
    key_noise = jax.random.fold_in(key, 0)
    noise = jnp.clip(jax.random.normal(key_noise, (3, D, D), jnp.float32), -4.0, 4.0) * D ** (-0.5)
    return noise.astype(jnp.bfloat16)


def touch_ends(values, rng, least, top_value):
    spot = [jax.random.randint(jax.random.fold_in(rng, axis), (), 0, length) for axis, length in enumerate(values.shape)]
    widest = values.shape.index(max(values.shape))
    neighbour = spot[:widest] + [(spot[widest] + 1) % values.shape[widest]] + spot[widest + 1:]
    return values.at[tuple(spot)].set(least).at[tuple(neighbour)].set(top_value)


def levels(rng, extent, cuts, low, largest):
    level = 1.0
    for position, blocks in cuts:
        steps = jax.random.uniform(jax.random.fold_in(jax.random.fold_in(rng, 6), position), (blocks,), jnp.float32, low / len(cuts), largest / len(cuts))
        level = level * jnp.repeat(jnp.exp(steps), extent[position] // blocks).reshape((-1,) + (1,) * (len(extent) - 1 - position))
    return level


def bell_draw(stream_key, extent, spread, bound, cuts=(), kind=jnp.bfloat16):
    loudness = levels(stream_key, extent, cuts, -0.22, 0.18) if cuts else 1.0
    entries = jax.random.normal(stream_key, extent, jnp.float32) * spread * loudness
    return jnp.minimum(jnp.maximum(entries, -bound), bound).astype(kind)


def setup_inputs(seed: int = 0) -> dict:
    splits = jax.random.split(jax.random.key(seed), 6)
    tokens = bell_draw(splits[0], (NLAT, NLON, LEV, D), 1.0, 6.0, ((0, 2), (1, 32), (2, 2)))
    land_mask = touch_ends((jax.random.randint(splits[1], (NLAT, NLON, LEV), 0, 4) < 3).astype(jnp.int32), jax.random.fold_in(splits[1], 1), 0, 1)
    qkv_weight = draw_qkv_weight(jax.random.fold_in(splits[5], 71), 0)
    out_weight = bell_draw(splits[3], (D, D), D ** -0.5, 0.1875, ((0, 2),))
    out_grad = bell_draw(splits[4], (NLAT, NLON, LEV, D), 1.0, 6.0, ((0, 2), (1, 32), (2, 2)))
    return {"tokens": tokens, "land_mask": land_mask, "qkv_weight": qkv_weight, "out_weight": out_weight, "out_grad": out_grad}


def window_split(grid):
    lat_rows, lon_cols = (grid.shape[0], grid.shape[1])
    tail = grid.shape[2:]
    grid = grid.reshape((lat_rows // WIN_LAT, WIN_LAT, lon_cols // WIN_LON, WIN_LON) + tail)
    grid = jnp.moveaxis(grid, 2, 1)
    return grid.reshape((lat_rows // WIN_LAT * (lon_cols // WIN_LON), WIN_LAT * WIN_LON * tail[0]) + tail[1:])

def window_merge(blocks, lat_rows, lon_cols):
    tail = blocks.shape[2:]
    blocks = blocks.reshape((lat_rows // WIN_LAT, lon_cols // WIN_LON, WIN_LAT, WIN_LON, LEV) + tail)
    blocks = jnp.moveaxis(blocks, 2, 1)
    return blocks.reshape((lat_rows, lon_cols, LEV) + tail)

def window_grads(token_win, mask_win, region_win, grad_win, qkv_weight, out_weight):
    f32 = jnp.float32
    nwin, seq = (token_win.shape[0], token_win.shape[1])
    width = qkv_weight.shape[2]
    head_count = width // HEAD_DIM
    scale = HEAD_DIM ** (-0.5)
    features = token_win.astype(f32)
    mean_removed = features - lax.optimization_barrier(jnp.mean(features, axis=-1, keepdims=True))
    variance = lax.optimization_barrier(jnp.mean(mean_removed * mean_removed, axis=-1, keepdims=True))
    inverse_deviation = lax.rsqrt(variance + 1e-05)
    standardized_input = mean_removed * inverse_deviation
    normalized_tokens = standardized_input.astype(jnp.bfloat16)
    projected = jnp.einsum('wsd,jde->jwse', normalized_tokens.astype(f32), qkv_weight.astype(f32)).astype(jnp.bfloat16)
    heads = projected.reshape(3, nwin, seq, head_count, HEAD_DIM)
    queries, key_rows, value_rows = (heads[0], heads[1], heads[2])
    scores = jnp.einsum('wshe,wthe->whst', queries.astype(f32), key_rows.astype(f32)) * scale
    same_region = region_win[:, :, None] == region_win[:, None, :]
    diagonal = jnp.eye(seq, dtype=bool)[None]
    permitted_pairs = same_region & ((mask_win[:, None, :] == 1) | diagonal)
    scores = jnp.where(permitted_pairs[:, None], scores, -1e+30)
    top_score = lax.optimization_barrier(jnp.max(scores, axis=-1, keepdims=True))
    expo = jnp.exp(scores - top_score)
    prob_f32 = expo / lax.optimization_barrier(jnp.sum(expo, axis=-1, keepdims=True))
    prob_bf16 = prob_f32.astype(jnp.bfloat16)
    attended = jnp.einsum('whst,wthe->wshe', prob_bf16.astype(f32), value_rows.astype(f32)).astype(jnp.bfloat16)
    attended = attended.reshape(nwin, seq, width)
    d_out_weight = jnp.einsum('wse,wsd->ed', attended.astype(f32), grad_win.astype(f32))
    d_attended = jnp.einsum('wsd,ed->wse', grad_win.astype(f32), out_weight.astype(f32)).astype(jnp.bfloat16)
    d_attended = d_attended.reshape(nwin, seq, head_count, HEAD_DIM)
    d_prob = jnp.einsum('wshe,wthe->whst', d_attended.astype(f32), value_rows.astype(f32))
    d_value = jnp.einsum('whst,wshe->wthe', prob_bf16.astype(f32), d_attended.astype(f32)).astype(jnp.bfloat16)
    d_scores = prob_f32 * (d_prob - lax.optimization_barrier(jnp.sum(prob_f32 * d_prob, axis=-1, keepdims=True))) * scale
    d_scores = d_scores.astype(jnp.bfloat16)
    d_query = jnp.einsum('whst,wthe->wshe', d_scores.astype(f32), key_rows.astype(f32)).astype(jnp.bfloat16)
    d_key = jnp.einsum('whst,wshe->wthe', d_scores.astype(f32), queries.astype(f32)).astype(jnp.bfloat16)
    d_proj = jnp.stack([d_query, d_key, d_value]).reshape(3, nwin, seq, width)
    d_qkv_weight = jnp.einsum('wsd,jwse->jde', normalized_tokens.astype(f32), d_proj.astype(f32))
    normalized_gradient = jnp.einsum('jwse,jde->wsd', d_proj.astype(f32), qkv_weight.astype(f32))
    shifted_gradient = inverse_deviation * (normalized_gradient - lax.optimization_barrier(jnp.mean(normalized_gradient, axis=-1, keepdims=True)) - standardized_input * lax.optimization_barrier(jnp.mean(normalized_gradient * standardized_input, axis=-1, keepdims=True)))
    return (shifted_gradient, d_qkv_weight, d_out_weight)

def reference(tokens, land_mask, qkv_weight, out_weight, out_grad):
    lat_total = tokens.shape[0]
    lon_total = tokens.shape[1]
    rolled_tokens = jnp.roll(tokens, (-SHIFT_LAT, -SHIFT_LON), (0, 1))
    rolled_mask = jnp.roll(land_mask, (-SHIFT_LAT, -SHIFT_LON), (0, 1))
    rolled_grad = jnp.roll(out_grad, (-SHIFT_LAT, -SHIFT_LON), (0, 1))
    row_ids = jnp.arange(lat_total, dtype=jnp.int32)
    region_rows = ((row_ids + SHIFT_LAT) % lat_total < SHIFT_LAT).astype(jnp.int32)
    nbands = lat_total // WIN_LAT

    def band_step(carry, band):
        start = (band * WIN_LAT).astype(jnp.int32)
        band_tokens = lax.dynamic_slice_in_dim(rolled_tokens, start, WIN_LAT, 0)
        band_mask = lax.dynamic_slice_in_dim(rolled_mask, start, WIN_LAT, 0)
        band_grad = lax.dynamic_slice_in_dim(rolled_grad, start, WIN_LAT, 0)
        band_region = lax.dynamic_slice_in_dim(region_rows, start, WIN_LAT, 0)
        region_grid = jnp.broadcast_to(band_region[:, None, None], (WIN_LAT, lon_total, LEV))
        shifted_gradient, d_qkv, d_out = window_grads(window_split(band_tokens), window_split(band_mask), window_split(region_grid), window_split(band_grad), qkv_weight, out_weight)
        return ((carry[0] + d_qkv, carry[1] + d_out), window_merge(shifted_gradient, WIN_LAT, lon_total))
    init = (jnp.zeros(qkv_weight.shape, jnp.float32), jnp.zeros(out_weight.shape, jnp.float32))
    (d_qkv_weight, d_out_weight), bands = lax.scan(band_step, init, jnp.arange(nbands, dtype=jnp.int32))
    shifted_gradient = bands.reshape((lat_total, lon_total, LEV, tokens.shape[3]))
    d_tokens = (jnp.roll(shifted_gradient, (SHIFT_LAT, SHIFT_LON), (0, 1)) + out_grad.astype(jnp.float32)).astype(jnp.bfloat16)
    return (d_tokens, d_qkv_weight, d_out_weight)
```

```python
import jax
import jax.numpy as jnp
from jax import lax
from jax.experimental import pallas as pl
from jax.experimental.pallas import tpu as pltpu
from jax.sharding import PartitionSpec as P

HEAD_DIM = 64
LEV = 2
WIN_LAT = 6
WIN_LON = 12
SHIFT_LAT = 3
SHIFT_LON = 6


def shifted(block, axis, distance):
    devices = range(lax.axis_size(axis))
    route = [((i - distance) % len(devices), i) for i in devices]
    return lax.ppermute(block, axis, route)


def shortened(array):
    return jax.tree.map(lambda a: a.astype(jnp.bfloat16) if a.dtype == jnp.float32 else a, array)


def window_split(grid):
    lat_rows, lon_cols = (grid.shape[0], grid.shape[1])
    tail = grid.shape[2:]
    grid = grid.reshape((lat_rows // WIN_LAT, WIN_LAT, lon_cols // WIN_LON, WIN_LON) + tail)
    grid = jnp.moveaxis(grid, 2, 1)
    return grid.reshape(
        (lat_rows // WIN_LAT * (lon_cols // WIN_LON), WIN_LAT * WIN_LON * tail[0]) + tail[1:]
    )


def window_merge(blocks, lat_rows, lon_cols):
    tail = blocks.shape[2:]
    blocks = blocks.reshape(
        (lat_rows // WIN_LAT, lon_cols // WIN_LON, WIN_LAT, WIN_LON, LEV) + tail
    )
    blocks = jnp.moveaxis(blocks, 2, 1)
    return blocks.reshape((lat_rows, lon_cols, LEV) + tail)


def window_grads(token_win, mask_win, region_win, grad_win, qkv_weight, out_weight):
    f32 = jnp.float32
    nwin, seq = (token_win.shape[0], token_win.shape[1])
    width = qkv_weight.shape[2]
    head_count = width // HEAD_DIM
    scale = HEAD_DIM ** (-0.5)
    features = token_win.astype(f32)
    mean_removed = features - jnp.mean(features, axis=-1, keepdims=True)
    variance = jnp.mean(mean_removed * mean_removed, axis=-1, keepdims=True)
    inverse_deviation = lax.rsqrt(variance + 1e-05)
    standardized_input = mean_removed * inverse_deviation
    normalized_tokens = standardized_input.astype(jnp.bfloat16)
    projected = jnp.einsum(
        "wsd,jde->jwse", normalized_tokens, qkv_weight, preferred_element_type=f32
    ).astype(jnp.bfloat16)
    heads = projected.reshape(3, nwin, seq, head_count, HEAD_DIM)
    queries, key_rows, value_rows = (heads[0], heads[1], heads[2])
    scores = jnp.einsum("wshe,wthe->whst", queries, key_rows, preferred_element_type=f32) * scale
    same_region = region_win[:, :, None] == region_win[:, None, :]
    diagonal = jnp.eye(seq, dtype=bool)[None]
    permitted_pairs = same_region & ((mask_win[:, None, :] == 1) | diagonal)
    scores = jnp.where(permitted_pairs[:, None], scores, -1e30)
    top_score = jnp.max(scores, axis=-1, keepdims=True)
    expo = jnp.exp(scores - top_score)
    prob_f32 = expo / jnp.sum(expo, axis=-1, keepdims=True)
    prob_bf16 = prob_f32.astype(jnp.bfloat16)
    attended = jnp.einsum(
        "whst,wthe->wshe", prob_bf16, value_rows, preferred_element_type=f32
    ).astype(jnp.bfloat16)
    attended = attended.reshape(nwin, seq, width)
    d_out_weight = jnp.einsum("wse,wsd->de", attended, grad_win, preferred_element_type=f32)
    d_attended = jnp.einsum("wsd,ed->wse", grad_win, out_weight, preferred_element_type=f32).astype(
        jnp.bfloat16
    )
    d_attended = d_attended.reshape(nwin, seq, head_count, HEAD_DIM)
    d_prob = jnp.einsum("wshe,wthe->whst", d_attended, value_rows, preferred_element_type=f32)
    d_value = jnp.einsum(
        "whst,wshe->wthe", prob_bf16, d_attended, preferred_element_type=f32
    ).astype(jnp.bfloat16)
    d_scores = prob_f32 * (d_prob - jnp.sum(prob_f32 * d_prob, axis=-1, keepdims=True)) * scale
    d_scores = d_scores.astype(jnp.bfloat16)
    d_query = jnp.einsum("whst,wthe->wshe", d_scores, key_rows, preferred_element_type=f32).astype(
        jnp.bfloat16
    )
    d_key = jnp.einsum("whst,wshe->wthe", d_scores, queries, preferred_element_type=f32).astype(
        jnp.bfloat16
    )
    d_proj = jnp.stack([d_query, d_key, d_value]).reshape(3, nwin, seq, width)
    d_qkv_weight = jnp.einsum(
        "wsd,jwse->jde", normalized_tokens, d_proj, preferred_element_type=f32
    )
    normalized_gradient = jnp.einsum(
        "jwse,jde->wsd", d_proj, qkv_weight, preferred_element_type=f32
    )
    shifted_gradient = inverse_deviation * (
        normalized_gradient
        - jnp.mean(normalized_gradient, axis=-1, keepdims=True)
        - standardized_input
        * jnp.mean(normalized_gradient * standardized_input, axis=-1, keepdims=True)
    )
    return (shifted_gradient, d_qkv_weight, d_out_weight)


def place():
    lat, lon, tp = (lax.axis_index(a) for a in ("lat", "lon", "tp"))
    return lon // 8, (lon // 2) % 4, (lon % 2) * 2 + lat, tp


def device_at(y, x, z, tp):
    return (z % 2, (y * 4 + x) * 2 + z // 2, tp)


def reduce_peers():
    y, x, z, tp = place()
    along_y = [device_at((y + d) % 4, x, z, tp) for d in (1, 2, 3)]
    along_x = [device_at(y, (x + d) % 4, z, tp) for d in (1, 2, 3)]
    along_z = [device_at(y, x, (z + d) % 4, tp) for d in (1, 2, 3)]
    return along_y, along_x, along_z


def reduce_kernel(grads, out, got1, mid1, got2, mid2, got3, send_sem, recv_sem):
    y, x, z, tp = place()
    along_y, along_x, along_z = reduce_peers()
    barrier = pltpu.get_barrier_semaphore()
    for peer in along_y + along_x + along_z:
        pl.semaphore_signal(barrier, inc=1, device_id=peer, device_id_type=pl.DeviceIdType.MESH)
    pl.semaphore_wait(barrier, 9)

    def copy(src, dst, color, stage, slot, peer):
        return pltpu.make_async_remote_copy(
            src_ref=src,
            dst_ref=dst,
            send_sem=send_sem.at[color, stage, slot],
            recv_sem=recv_sem.at[color, stage, slot],
            device_id=peer,
            device_id_type=pl.DeviceIdType.MESH,
        )

    first, second = ((y, x), (x, y))
    peers = ((along_y, along_x), (along_x, along_y))
    copies1 = []
    for color in (0, 1):
        copies1.append(
            [
                copy(
                    grads.at[color, :, (first[color] + d) % 4],
                    got1.at[color, d - 1],
                    color, 0, d - 1, peers[color][0][d - 1],
                )
                for d in (1, 2, 3)
            ]
        )
        for c in copies1[color]:
            c.start()
    copies2 = []
    for color in (0, 1):
        for c in copies1[color]:
            c.wait_recv()
        for m in range(2):
            for b in range(4):
                total = grads[color, m, first[color], b].astype(jnp.float32)
                for d in range(3):
                    total += got1[color, d, m, b].astype(jnp.float32)
                mid1[color, m, b] = total.astype(jnp.bfloat16)
        copies2.append(
            [
                copy(
                    mid1.at[color, :, (second[color] + d) % 4],
                    got2.at[color, d - 1],
                    color, 1, d - 1, peers[color][1][d - 1],
                )
                for d in (1, 2, 3)
            ]
        )
        for c in copies2[color]:
            c.start()
    copies3 = []
    for color in (0, 1):
        for c in copies2[color]:
            c.wait_recv()
        for m in range(2):
            total = mid1[color, m, second[color]].astype(jnp.float32)
            for d in range(3):
                total += got2[color, d, m].astype(jnp.float32)
            total = total.astype(jnp.bfloat16)
            mid2[color, 0, m] = total[:32]
            mid2[color, 1, m] = total[32:]
        for m in range(2):
            got3[z, color, m] = mid2[color, z // 2, m]
        copies3.append(
            [
                copy(
                    mid2.at[color, ((z + d) % 4) // 2],
                    got3.at[z, color],
                    color, 2, d - 1, along_z[d - 1],
                )
                for d in (1, 2, 3)
            ]
        )
        for c in copies3[color]:
            c.start()
    for color in (0, 1):
        for c in copies3[color]:
            c.wait_recv()
        for m in range(2):
            total = got3[0, color, m].astype(jnp.float32)
            for i in range(1, 4):
                total += got3[i, color, m].astype(jnp.float32)
            out[2 * color + m] = total
    for group in copies1 + copies2 + copies3:
        for c in group:
            c.wait_send()


def reduce_weights(grads):
    cols = grads.shape[-1]
    bf16 = jnp.bfloat16
    return pl.pallas_call(
        reduce_kernel,
        out_shape=jax.ShapeDtypeStruct((4, 32, cols), jnp.float32),
        in_specs=[pl.BlockSpec(memory_space=pltpu.VMEM)],
        out_specs=pl.BlockSpec(memory_space=pltpu.VMEM),
        scratch_shapes=[
            pltpu.VMEM((2, 3, 2, 4, 64, cols), bf16),
            pltpu.VMEM((2, 2, 4, 64, cols), bf16),
            pltpu.VMEM((2, 3, 2, 64, cols), bf16),
            pltpu.VMEM((2, 2, 2, 32, cols), bf16),
            pltpu.VMEM((4, 2, 2, 32, cols), bf16),
            pltpu.SemaphoreType.DMA((2, 3, 3)),
            pltpu.SemaphoreType.DMA((2, 3, 3)),
        ],
        compiler_params=pltpu.CompilerParams(
            collective_id=0, has_side_effects=True, vmem_limit_bytes=48 * 1024 * 1024
        ),
        name="reduce_weights",
    )(grads)


def body(tokens, land_mask, qkv_weight, out_weight, out_grad):
    rows_dev, cols_dev = (tokens.shape[0], tokens.shape[1])
    own_arrays = (tokens, land_mask, out_grad)
    upper_rims = shifted(
        (tokens[:SHIFT_LAT], land_mask[:SHIFT_LAT], out_grad[:SHIFT_LAT]), "lat", -1
    )
    rolled_rows = tuple(
        (
            jnp.concatenate([whole_part[SHIFT_LAT:], extra_part], axis=0)
            for whole_part, extra_part in zip(own_arrays, upper_rims)
        )
    )
    column_rims = shifted(
        (
            rolled_rows[0][:, :SHIFT_LON],
            shortened(rolled_rows[1][:, :SHIFT_LON]),
            rolled_rows[2][:, :SHIFT_LON],
        ),
        "lon",
        -1,
    )
    rolled_all = tuple(
        (
            jnp.concatenate([whole_part[:, SHIFT_LON:], extra_part], axis=1)
            for whole_part, extra_part in zip(rolled_rows, column_rims)
        )
    )
    full_tokens, full_mask, full_grad = (
        lax.all_gather(rolled_all[0], "tp", axis=2, tiled=True),
        lax.all_gather(shortened(rolled_all[1]), "tp", axis=2, tiled=True),
        lax.all_gather(rolled_all[2], "tp", axis=2, tiled=True),
    )
    lat_total = rows_dev * lax.axis_size("lat")
    row_ids = lax.axis_index("lat") * rows_dev + jnp.arange(rows_dev, dtype=jnp.int32)
    region_rows = ((row_ids + SHIFT_LAT) % lat_total < SHIFT_LAT).astype(jnp.int32)
    region_grid = jnp.broadcast_to(
        region_rows[:, None, None], (rows_dev, cols_dev, full_mask.shape[2])
    )
    shifted_gradient, d_qkv, d_out = window_grads(
        window_split(full_tokens),
        window_split(full_mask),
        window_split(region_grid),
        window_split(full_grad),
        qkv_weight,
        out_weight,
    )
    partial_grid = window_merge(shifted_gradient, rows_dev, cols_dev)
    shares = lax.psum_scatter(
        partial_grid.astype(jnp.bfloat16), "tp", scatter_dimension=2, tiled=True
    ).astype(jnp.float32)
    column_back = shifted(shares[:, cols_dev - SHIFT_LON :].astype(jnp.bfloat16), "lon", 1).astype(
        jnp.float32
    )
    shares = jnp.concatenate([column_back, shares[:, : cols_dev - SHIFT_LON]], axis=1)
    row_back = shifted(shares[rows_dev - SHIFT_LAT :].astype(jnp.bfloat16), "lat", 1).astype(
        jnp.float32
    )
    shares = jnp.concatenate([row_back, shares[: rows_dev - SHIFT_LAT]], axis=0)
    d_tokens = (shares + out_grad.astype(jnp.float32)).astype(jnp.bfloat16)
    width = d_out.shape[1]
    blocks = jnp.concatenate([d_qkv, d_out[None]]).astype(jnp.bfloat16)
    blocks = blocks.reshape(2, 2, 4, 4, 64, width)
    blocks = jnp.stack([blocks[0], jnp.swapaxes(blocks[1], 1, 2)])
    reduced = reduce_weights(blocks)
    d_qkv_weight, d_out_weight = reduced[:3], reduced[3].T
    return (d_tokens, d_qkv_weight, d_out_weight)


def solution(mesh):
    in_specs = (
        P("lat", "lon", "tp", None),
        P("lat", "lon", "tp"),
        P(None, None, "tp"),
        P("tp", None),
        P("lat", "lon", "tp", None),
    )
    out_specs = (P("lat", "lon", "tp", None), P(None, "lon", "tp"), P("tp", "lon"))
    return jax.shard_map(body, mesh=mesh, in_specs=in_specs, out_specs=out_specs, check_vma=False)
```

```python
import jax
import jax.numpy as jnp
import numpy as np
from jax import lax
from jax.experimental import pallas as pl
from jax.experimental.pallas import tpu as pltpu
from jax.sharding import PartitionSpec as P

f32, bf16 = jnp.float32, jnp.bfloat16
MESH = pl.DeviceIdType.MESH
NN = (((1,), (0,)), ((), ()))
NT = (((1,), (1,)), ((), ()))

D = 1024
HEADS = 4
GROUP = HEADS * 64
PASSES = 2
ROWS = COLS = 24
OWN = ROWS * COLS
WINDOWS = 8
LEVEL = 72
SEQ = 2 * LEVEL
SLOT = 80
LOCAL = 3
WIDE = D + 128
A_ROWS, C_ROWS, B_ROWS = 128, 32, 64
HALO = A_ROWS + C_ROWS + B_ROWS
PARTS = ((0, A_ROWS), (A_ROWS, C_ROWS), (A_ROWS + C_ROWS, B_ROWS))
BAND_START = (64, 208, 352, 416)


def selections():
    send = np.zeros((HALO, OWN), np.float32)
    for r in range(ROWS):
        for c in range(COLS):
            if r >= 3 and c < 6:
                send[(r - 3) * 6 + c, r * COLS + c] = 1
            elif r < 3 and c < 6:
                send[A_ROWS + r * 6 + c, r * COLS + c] = 1
            elif r < 3:
                send[A_ROWS + C_ROWS + r * 18 + c - 6, r * COLS + c] = 1
    own = np.zeros((WINDOWS, SLOT, 160), np.float32)
    halo = np.zeros((WINDOWS, SLOT, HALO), np.float32)
    for j in range(2):
        for b in range(4):
            w = j * 4 + b
            for i in range(6):
                for c in range(12):
                    t, r, col = i * 12 + c, 6 * b + i, 12 * j + c
                    if r < 21 and col < 18:
                        own[w, t, (r + 3) * COLS + col + 6 - BAND_START[b]] = 1
                    elif r < 21:
                        halo[w, t, r * 6 + col - 18] = 1
                    elif col >= 18:
                        halo[w, t, A_ROWS + (r - 21) * 6 + col - 18] = 1
                    else:
                        halo[w, t, A_ROWS + C_ROWS + (r - 21) * 18 + col] = 1
    own = own[[0, 3, 4, 7]]
    halo = halo[3:]
    swap = lambda a: np.ascontiguousarray(np.swapaxes(a, -1, -2))
    return [a.astype(jnp.bfloat16) for a in (send, swap(send), own, swap(own), halo, swap(halo))]


def own_kind(w):
    return (0, 0, 0, 1, 2, 2, 2, 3)[w]


def dot(a, b, dims=NN):
    return lax.dot_general(a, b, dims, preferred_element_type=f32)


def place():
    lat, lon, tp = (lax.axis_index(a) for a in ("lat", "lon", "tp"))
    return lon // 8, (lon // 2) % 4, (lon % 2) * 2 + lat, tp


def device_at(y, x, z, tp):
    return (z % 2, (y * 4 + x) * 2 + z // 2, tp)


def kernel(
    x, g, mask, wq, wo, send_m, send_t, own_m, own_t, halo_m, halo_t,
    dtok, dw,
    nat, mean, rstd, out_n, out_g, in_n, in_g, nw, gw, nf, gf, n_t, g_t, bias, qkv, da, att, dp,
    grads, got1, mid1, got2, mid2, got3,
    mine, back_out, back_in, total, ret_out, ret_in, local,
    halo_s, halo_r, core_s, core_r, ret_s, ret_r, back_s, back_r, red_s, red_r,
):
    y, px, z, tp = place()
    lat, lon = lax.axis_index("lat"), lax.axis_index("lon")
    other = (lat, lon, 1 - tp)
    before, after = (lon + 31) % 32, (lon + 1) % 32
    along_y = [device_at((y + d) % 4, px, z, tp) for d in (1, 2, 3)]
    along_x = [device_at(y, (px + d) % 4, z, tp) for d in (1, 2, 3)]
    along_z = [device_at(y, px, (z + d) % 4, tp) for d in (1, 2, 3)]
    to_a, to_c, to_b = (lat, before, tp), (1 - lat, before, tp), (1 - lat, lon, tp)
    from_a, from_c = (lat, after, tp), (1 - lat, after, tp)

    barrier = pltpu.get_barrier_semaphore()
    greeted = [other, to_a, to_c, from_a, from_c] + along_y + along_x + along_z
    for peer in greeted:
        pl.semaphore_signal(barrier, inc=1, device_id=peer, device_id_type=MESH)

    def copy(src, dst, s, r, peer):
        return pltpu.make_async_remote_copy(
            src_ref=src, dst_ref=dst, send_sem=s, recv_sem=r, device_id=peer, device_id_type=MESH
        )

    @pl.loop(0, OWN // 64)
    def _(i):
        rows = pl.ds(pl.multiple_of(i * 64, 64), 64)
        v = x[rows, :].astype(f32)
        m = jnp.mean(v, axis=-1, keepdims=True)
        v = v - m
        s = lax.rsqrt(jnp.mean(v * v, axis=-1, keepdims=True) + 1e-05)
        mean[rows, :] = m
        rstd[rows, :] = s
        nat[rows, :D] = (v * s).astype(bf16)
        nat[rows, D:] = mask[rows, :]

    out_n[...] = dot(send_m[...], nat[...]).astype(bf16)
    out_g[...] = dot(send_m[...], g[...]).astype(bf16)
    pl.semaphore_wait(barrier, len(greeted))

    halos = []
    for i, ((start, size), peer) in enumerate(zip(PARTS, (to_a, to_c, to_b))):
        rows = pl.ds(start, size)
        halos.append(copy(out_n.at[rows], in_n.at[rows], halo_s.at[0, i], halo_r.at[0, i], peer))
        halos.append(copy(out_g.at[rows], in_g.at[rows], halo_s.at[1, i], halo_r.at[1, i], peer))
    for c in halos:
        c.start()

    def exchanges(w):
        return (
            copy(nw.at[tp, w], nw.at[tp, w], core_s.at[0, w], core_r.at[0, w], other),
            copy(gw.at[tp, w], gw.at[tp, w], core_s.at[1, w], core_r.at[1, w], other),
        )

    def assemble(w):
        rows = pl.ds(BAND_START[w % 4], 160)
        n, c = dot(own_m[own_kind(w)], nat[rows, :]), dot(own_m[own_kind(w)], g[rows, :])
        if w >= LOCAL:
            n += dot(halo_m[w - LOCAL], in_n[...])
            c += dot(halo_m[w - LOCAL], in_g[...])
        nw[tp, w] = n.astype(bf16)
        gw[tp, w] = c.astype(bf16)
        for e in exchanges(w):
            e.start()

    def gather(w):
        for e in exchanges(w):
            e.wait_recv()
        rows = pl.ds(pl.multiple_of(w * SEQ, 16), SEQ)
        n = jnp.concatenate([nw[i, w].astype(f32)[:LEVEL] for i in (0, 1)])
        nf[rows, :] = n[:, :D].astype(bf16)
        gf[rows, :] = jnp.concatenate([gw[i, w].astype(f32)[:LEVEL] for i in (0, 1)]).astype(bf16)
        keys = jnp.concatenate([n[:, D:], n[:, D : D + SEQ - 128]], axis=1)
        t = lax.broadcasted_iota(jnp.int32, (SEQ, SEQ), 0)
        s = lax.broadcasted_iota(jnp.int32, (SEQ, SEQ), 1)
        region = lambda i: jnp.where(i >= LEVEL, i - LEVEL, i) >= LEVEL // 2
        last = ((w % 4) == 3).astype(jnp.int32) * lat
        crossing = jnp.where(region(t) != region(s), 1, 0) * last
        open_key = jnp.where(t == s, 1.0, keys)
        bias[w] = jnp.where((open_key == 1.0) & (crossing == 0), 0.0, -1e30)

    def project(p, start, size):
        rows, c = pl.ds(start, size), pl.ds(p * GROUP, GROUP)
        n = nf[rows, :]
        for j in range(3):
            o = dot(n, wq[j, :, c]).astype(bf16)
            qkv[j, rows, :] = o * bf16(0.125) if j == 0 else o
        da[rows, :] = dot(gf[rows, :], wo[c, :], NT).astype(bf16)

    lane = lax.broadcasted_iota(jnp.int32, (1, GROUP), 1) // 64
    heads = [(lane == h).astype(f32).astype(bf16) for h in range(HEADS)]

    def attend(p, w):
        rows, c = pl.ds(pl.multiple_of(w * SEQ, 16), SEQ), pl.ds(p * GROUP, GROUP)
        q, k, v, d = qkv[0, rows, :], qkv[1, rows, :], qkv[2, rows, :], da[rows, :]
        b = bias[w]
        v_t, k_t = v.T, k.T
        scores = dot(jnp.concatenate([k * m for m in heads]), q, NT)
        d_probs = dot(jnp.concatenate([v * m for m in heads]), d, NT)
        d_v, d_k = jnp.zeros((SEQ, GROUP), f32), jnp.zeros((SEQ, GROUP), f32)
        out_t, d_q_t = [], []
        for h in range(HEADS):
            s = scores[SEQ * h : SEQ * h + SEQ] + b
            e = jnp.exp(s - jnp.max(s, axis=0, keepdims=True))
            pr = e * (1.0 / jnp.sum(e, axis=0, keepdims=True))
            pb = pr.astype(bf16)
            u = pr * d_probs[SEQ * h : SEQ * h + SEQ]
            ds = (u - pr * jnp.sum(u, axis=0, keepdims=True)).astype(bf16)
            out_t.append(dot(v_t[64 * h : 64 * h + 64], pb))
            d_q_t.append(dot(k_t[64 * h : 64 * h + 64], ds))
            d_v += dot(pb, d * heads[h])
            d_k += dot(ds, q * heads[h])
        att[rows, c] = jnp.concatenate(out_t).astype(bf16).T
        dp[0, rows, c] = (jnp.concatenate(d_q_t) * 0.125).astype(bf16).T
        dp[1, rows, c] = d_k.astype(bf16)
        dp[2, rows, c] = d_v.astype(bf16)

    first, second = (y, px), (px, y)
    peers = ((along_y, along_x), (along_x, along_y))

    def stage(n, p, color, d):
        sems = (red_s.at[p, color, n, d - 1], red_r.at[p, color, n, d - 1])
        if n == 0:
            src = grads.at[p, color, (first[color] + d) % 4]
            return copy(src, got1.at[p, color, d - 1], *sems, peers[color][0][d - 1])
        if n == 1:
            src = mid1.at[p, color, (second[color] + d) % 4]
            return copy(src, got2.at[p, color, d - 1], *sems, peers[color][1][d - 1])
        src = mid2.at[p, color, ((z + d) % 4) // 2]
        return copy(src, got3.at[p, z, color], *sems, along_z[d - 1])

    def weight_grads(p):
        c = pl.ds(p * GROUP, GROUP)
        for d in (1, 2, 3, 0):
            row = (y + d) % 4
            a = n_t[pl.ds(pl.multiple_of(row * 256, 256), 256), :]
            col = (px + d) % 4
            pieces = [pl.ds(pl.multiple_of(i * 256 + col * 64, 64), 64) for i in range(4)]
            b = jnp.concatenate([n_t[i, :] for i in pieces])
            e = jnp.concatenate([g_t[i, :] for i in pieces])
            for color, m, val in (
                (0, 0, dot(a, dp[0, :, c])),
                (0, 1, dot(a, dp[1, :, c])),
                (1, 0, dot(b, dp[2, :, c])),
                (1, 1, dot(e, att[:, c])),
            ):
                val = val.astype(bf16)
                for i in range(4):
                    grads[p, color, (row, col)[color], i, m] = val[64 * i : 64 * i + 64]
            if d:
                stage(0, p, 0, d).start()
                stage(0, p, 1, d).start()

    def reduce_first(p):
        for color in (0, 1):
            for d in (1, 2, 3):
                stage(0, p, color, d).wait_recv()

            @pl.loop(0, 4)
            def _(i):
                s = grads[p, color, first[color], i].astype(f32)
                for d in range(3):
                    s += got1[p, color, d, i].astype(f32)
                mid1[p, color, i] = s.astype(bf16)

            for d in (1, 2, 3):
                stage(1, p, color, d).start()

    def reduce_second(p):
        for color in (0, 1):
            for d in (1, 2, 3):
                stage(1, p, color, d).wait_recv()
            s = mid1[p, color, second[color]].astype(f32)
            for d in range(3):
                s += got2[p, color, d].astype(f32)
            s = s.astype(bf16)
            mid2[p, color, 0] = s[:, :32]
            mid2[p, color, 1] = s[:, 32:]
            got3[p, z, color] = mid2[p, color, z // 2]
            for d in (1, 2, 3):
                stage(2, p, color, d).start()

    def reduce_third(p):
        for color in (0, 1):
            for d in (1, 2, 3):
                stage(2, p, color, d).wait_recv()
            s = got3[p, 0, color].astype(f32)
            for i in range(1, 4):
                s += got3[p, i, color].astype(f32)
            for m in range(2):
                dw[2 * color + m, :, p * GROUP : p * GROUP + GROUP] = s[m]

    for w in range(LOCAL):
        assemble(w)
    pl.loop(0, LOCAL)(gather)
    for p in range(PASSES):
        project(p, 0, LOCAL * SEQ)
        pl.loop(0, LOCAL)(lambda w, p=p: attend(p, w))
    for c in halos:
        c.wait_recv()
    for w in range(LOCAL, WINDOWS):
        assemble(w)
    pl.loop(LOCAL, WINDOWS)(gather)
    for i in range(9):
        rows = pl.ds(i * 128, 128)
        n_t[:, i * 128 : i * 128 + 128] = nf[rows, :].T
        g_t[:, i * 128 : i * 128 + 128] = gf[rows, :].T
    for p in range(PASSES):
        project(p, LOCAL * SEQ, (WINDOWS - LOCAL) * SEQ)
        pl.loop(LOCAL, WINDOWS)(lambda w, p=p: attend(p, w))
        if p:
            reduce_first(p - 1)
        weight_grads(p)
        if p:
            reduce_second(p - 1)

    def returned(w):
        return copy(back_out.at[w], back_in.at[w], back_s.at[w], back_r.at[w], other)

    def d_normed(w):
        rows = pl.ds(pl.multiple_of(w * SEQ, 16), SEQ)
        o = sum(dot(dp[j, rows, :], wq[j], NT) for j in range(3))
        pad = jnp.zeros((SLOT - LEVEL, D), f32)
        lo, hi = jnp.concatenate([o[:LEVEL], pad]), jnp.concatenate([o[LEVEL:], pad])
        mine[w] = jnp.where(tp == 0, lo, hi)
        back_out[w] = jnp.where(tp == 0, hi, lo).astype(bf16)
        returned(w).start()

    pl.loop(LOCAL, WINDOWS)(d_normed)
    pl.loop(0, LOCAL)(d_normed)
    reduce_first(PASSES - 1)

    def add(w):
        returned(w).wait_recv()
        total[w] = (mine[w] + back_in[w].astype(f32)).astype(bf16)

    pl.loop(LOCAL, WINDOWS)(add)
    ret_out[...] = sum(dot(halo_t[w - LOCAL], total[w]) for w in range(LOCAL, WINDOWS)).astype(bf16)
    returns = []
    for i, ((start, size), peer) in enumerate(zip(PARTS, (from_a, from_c, to_b))):
        rows = pl.ds(start, size)
        returns.append(copy(ret_out.at[rows], ret_in.at[rows], ret_s.at[i], ret_r.at[i], peer))
    for c in returns:
        c.start()
    pl.loop(0, LOCAL)(add)
    local[:LEVEL] = jnp.zeros((LEVEL, D), f32)
    for b in range(4):
        o = dot(own_t[own_kind(b)], total[b]) + dot(own_t[own_kind(b + 4)], total[b + 4])
        skip = 72 + 144 * b - BAND_START[b]
        size = 144 if b < 3 else 72
        local[72 + 144 * b : 72 + 144 * b + size] = o[skip : skip + size]
    reduce_second(PASSES - 1)
    for c in returns:
        c.wait_recv()

    @pl.loop(0, 4)
    def _(i):
        rows = pl.ds(pl.multiple_of(i * 144, 16), 144)
        dn = local[rows, :] + dot(send_t[rows, :], ret_in[...])
        s = rstd[rows, :]
        xh = (x[rows, :].astype(f32) - mean[rows, :]) * s
        inner = dn - jnp.mean(dn, axis=-1, keepdims=True) - xh * jnp.mean(dn * xh, axis=-1, keepdims=True)
        dtok[rows, :] = (s * inner + g[rows, :].astype(f32)).astype(bf16)

    for p in range(PASSES):
        reduce_third(p)
    for c in halos + returns:
        c.wait_send()

    @pl.loop(0, WINDOWS)
    def _(w):
        for e in exchanges(w):
            e.wait_send()
        returned(w).wait_send()

    for p in range(PASSES):
        for n in range(3):
            for color in (0, 1):
                for d in (1, 2, 3):
                    stage(n, p, color, d).wait_send()


def body(tokens, land_mask, qkv_weight, out_weight, out_grad):
    mask = jnp.broadcast_to(land_mask.reshape(OWN, 1).astype(bf16), (OWN, 128))
    constants = [jnp.asarray(a) for a in selections()]
    operands = [tokens.reshape(OWN, D), out_grad.reshape(OWN, D), mask, qkv_weight, out_weight] + constants
    vmem, dma = pltpu.VMEM, pltpu.SemaphoreType.DMA
    tokens_all = WINDOWS * SEQ
    d_tokens, d_weights = pl.pallas_call(
        kernel,
        out_shape=(jax.ShapeDtypeStruct((OWN, D), bf16), jax.ShapeDtypeStruct((4, 32, 512), f32)),
        in_specs=[pl.BlockSpec(memory_space=pltpu.VMEM)] * len(operands),
        out_specs=[pl.BlockSpec(memory_space=pltpu.VMEM)] * 2,
        scratch_shapes=[
            vmem((OWN, WIDE), bf16),
            vmem((OWN, 1), f32),
            vmem((OWN, 1), f32),
            vmem((HALO, WIDE), bf16),
            vmem((HALO, D), bf16),
            vmem((HALO, WIDE), bf16),
            vmem((HALO, D), bf16),
            vmem((2, WINDOWS, SLOT, WIDE), bf16),
            vmem((2, WINDOWS, SLOT, D), bf16),
            vmem((tokens_all, D), bf16),
            vmem((tokens_all, D), bf16),
            vmem((D, tokens_all), bf16),
            vmem((D, tokens_all), bf16),
            vmem((WINDOWS, SEQ, SEQ), f32),
            vmem((3, tokens_all, GROUP), bf16),
            vmem((tokens_all, GROUP), bf16),
            vmem((tokens_all, 512), bf16),
            vmem((3, tokens_all, 512), bf16),
            vmem((PASSES, 2, 4, 4, 2, 64, GROUP), bf16),
            vmem((PASSES, 2, 3, 4, 2, 64, GROUP), bf16),
            vmem((PASSES, 2, 4, 2, 64, GROUP), bf16),
            vmem((PASSES, 2, 3, 2, 64, GROUP), bf16),
            vmem((PASSES, 2, 2, 2, 32, GROUP), bf16),
            vmem((PASSES, 4, 2, 2, 32, GROUP), bf16),
            vmem((WINDOWS, SLOT, D), f32),
            vmem((WINDOWS, SLOT, D), bf16),
            vmem((WINDOWS, SLOT, D), bf16),
            vmem((WINDOWS, SLOT, D), bf16),
            vmem((HALO, D), bf16),
            vmem((HALO, D), bf16),
            vmem((OWN, D), f32),
            dma((2, 3)),
            dma((2, 3)),
            dma((2, WINDOWS)),
            dma((2, WINDOWS)),
            dma((3,)),
            dma((3,)),
            dma((WINDOWS,)),
            dma((WINDOWS,)),
            dma((PASSES, 2, 3, 3)),
            dma((PASSES, 2, 3, 3)),
        ],
        compiler_params=pltpu.CompilerParams(
            collective_id=0, has_side_effects=True, vmem_limit_bytes=63 * 1024 * 1024
        ),
        name="swin_backward",
    )(*operands)
    return d_tokens.reshape(ROWS, COLS, 1, D), d_weights[:3], d_weights[3].T


def solution(mesh):
    in_specs = (
        P("lat", "lon", "tp", None),
        P("lat", "lon", "tp"),
        P(None, None, "tp"),
        P("tp", None),
        P("lat", "lon", "tp", None),
    )
    out_specs = (P("lat", "lon", "tp", None), P(None, "lon", "tp"), P("tp", "lon"))
    return jax.shard_map(body, mesh=mesh, in_specs=in_specs, out_specs=out_specs, check_vma=False)
```

```python
import jax
import jax.numpy as jnp
import numpy as np
from jax import lax
from jax.experimental import pallas as pl
from jax.experimental.pallas import tpu as pltpu
from jax.sharding import PartitionSpec as P

f32, bf16 = jnp.float32, jnp.bfloat16
MESH = pl.DeviceIdType.MESH
NN = (((1,), (0,)), ((), ()))
NT = (((1,), (1,)), ((), ()))

D = 1024
HEADS = 4
GROUP = HEADS * 64
PASSES = 2
ROWS = COLS = 24
OWN = ROWS * COLS
WINDOWS = 8
LEVEL = 72
SEQ = 2 * LEVEL
SLOT = 80
EARLY = 4
WIDE = D + 128
A_ROWS, B_ROWS, C_ROWS = 128, 64, 32
BC_ROWS = B_ROWS + C_ROWS
HALO = A_ROWS + BC_ROWS
PARTS = ((0, A_ROWS), (A_ROWS, B_ROWS), (A_ROWS + B_ROWS, C_ROWS))
BAND_START = (64, 208, 352, 416)


def selections():
    send = np.zeros((HALO, OWN), np.float32)
    own = np.zeros((WINDOWS, SLOT, 160), np.float32)
    cols = np.zeros((4, SLOT, A_ROWS), np.float32)
    rest = np.zeros((2, SLOT, BC_ROWS), np.float32)
    for r in range(ROWS):
        for c in range(COLS):
            if r >= 3 and c < 6:
                send[(r - 3) * 6 + c, r * COLS + c] = 1
            elif r < 3 and c >= 6:
                send[A_ROWS + r * 18 + c - 6, r * COLS + c] = 1
            elif r < 3:
                send[A_ROWS + B_ROWS + r * 6 + c, r * COLS + c] = 1
    for j in range(2):
        for b in range(4):
            for i in range(6):
                for c in range(12):
                    t, r, col = i * 12 + c, 6 * b + i, 12 * j + c
                    if r < 21 and col < 18:
                        own[j * 4 + b, t, (r + 3) * COLS + col + 6 - BAND_START[b]] = 1
                    elif r < 21:
                        cols[b, t, r * 6 + col - 18] = 1
                    elif col < 18:
                        rest[j, t, (r - 21) * 18 + col] = 1
                    else:
                        rest[j, t, B_ROWS + (r - 21) * 6 + col - 18] = 1
    own = own[[0, 3, 4, 7]]
    swap = lambda a: np.ascontiguousarray(np.swapaxes(a, -1, -2))
    return [a.astype(jnp.bfloat16) for a in (send, swap(send), own, swap(own), cols, swap(cols), rest, swap(rest))]


def own_kind(w):
    return (0, 0, 0, 1, 2, 2, 2, 3)[w]


def dot(a, b, dims=NN):
    return lax.dot_general(a, b, dims, preferred_element_type=f32)


def place():
    lat, lon, tp = (lax.axis_index(a) for a in ("lat", "lon", "tp"))
    return lon // 8, (lon // 2) % 4, (lon % 2) * 2 + lat, tp


def device_at(y, x, z, tp):
    return (z % 2, (y * 4 + x) * 2 + z // 2, tp)


def kernel(
    x_h, g_h, mask, wq_h, wo_h, send_mh, send_th, own_mh, own_th, cols_mh, cols_th, rest_mh, rest_th,
    dtok, dwq, dwo,
    x, g, wq, wo, send_m, send_t, own_m, own_t, cols_m, cols_t, rest_m, rest_t,
    nat, mean, rstd, out_n, out_g, in_n, in_g, nw, gw, nf, gf, n_t, g_t, bias, qkv, da, att, dp,
    grads, half, got1, mid1, got2, mid2, got3,
    mine, back_out, total, ret_out, ret_in, local,
    load_s, halo_s, halo_r, core_s, core_r, ret_s, ret_r, back_s, back_r, half_s, half_r, red_s, red_r,
):
    y, px, z, tp = place()
    lat, lon = lax.axis_index("lat"), lax.axis_index("lon")
    other = (lat, lon, 1 - tp)
    before, after = (lon + 31) % 32, (lon + 1) % 32
    along_y = [device_at((y + d) % 4, px, z, tp) for d in (1, 2, 3)]
    along_x = [device_at(y, (px + d) % 4, z, tp) for d in (1, 2, 3)]
    along_z = [device_at(y, px, (z + d) % 4, tp) for d in (1, 2, 3)]
    to_a, to_b, to_c = (lat, before, tp), (1 - lat, lon, tp), (1 - lat, before, tp)
    from_a, from_c = (lat, after, tp), (1 - lat, after, tp)

    pairs = (
        (x_h, x), (send_mh, send_m), (g_h, g), (own_mh, own_m), (rest_mh, rest_m), (wq_h, wq), (wo_h, wo),
        (cols_mh, cols_m), (send_th, send_t), (own_th, own_t), (cols_th, cols_t), (rest_th, rest_t),
    )
    loads = [pltpu.make_async_copy(a, b, load_s.at[i]) for i, (a, b) in enumerate(pairs)]
    for c in loads:
        c.start()

    barrier = pltpu.get_barrier_semaphore()
    greeted = [other, to_a, to_c, from_a, from_c] + along_y + along_x + along_z
    for peer in greeted:
        pl.semaphore_signal(barrier, inc=1, device_id=peer, device_id_type=MESH)

    def copy(src, dst, s, r, peer):
        return pltpu.make_async_remote_copy(
            src_ref=src, dst_ref=dst, send_sem=s, recv_sem=r, device_id=peer, device_id_type=MESH
        )

    loads[0].wait()

    @pl.loop(0, OWN // 64)
    def _(i):
        rows = pl.ds(pl.multiple_of(i * 64, 64), 64)
        v = x[rows, :].astype(f32)
        m = jnp.mean(v, axis=-1, keepdims=True)
        v = v - m
        s = lax.rsqrt(jnp.mean(v * v, axis=-1, keepdims=True) + 1e-05)
        mean[rows, :] = m
        rstd[rows, :] = s
        nat[rows, :D] = (v * s).astype(bf16)
        nat[rows, D:] = mask[rows, :]

    for c in loads[1:5]:
        c.wait()
    out_g[...] = dot(send_m[...], g[...]).astype(bf16)
    out_n[...] = dot(send_m[...], nat[...]).astype(bf16)
    pl.semaphore_wait(barrier, len(greeted))

    halos = []
    for i, peer in ((1, to_b), (0, to_a), (2, to_c)):
        start, size = PARTS[i]
        rows = pl.ds(start, size)
        halos.append(copy(out_n.at[rows], in_n.at[rows], halo_s.at[0, i], halo_r.at[0, i], peer))
        halos.append(copy(out_g.at[rows], in_g.at[rows], halo_s.at[1, i], halo_r.at[1, i], peer))
    for c in halos:
        c.start()

    def exchanges(w):
        return (
            copy(nw.at[tp, w], nw.at[tp, w], core_s.at[0, w], core_r.at[0, w], other),
            copy(gw.at[tp, w], gw.at[tp, w], core_s.at[1, w], core_r.at[1, w], other),
        )

    def borrowed(w):
        if w == 3:
            return [(rest_m[0, :, :B_ROWS], A_ROWS, B_ROWS)]
        if w == 7:
            return [(cols_m[3], 0, A_ROWS), (rest_m[1], A_ROWS, BC_ROWS)]
        return [(cols_m[w - 4], 0, A_ROWS)] if w > 3 else []

    def assemble(w):
        rows = pl.ds(BAND_START[w % 4], 160)
        n, c = dot(own_m[own_kind(w)], nat[rows, :]), dot(own_m[own_kind(w)], g[rows, :])
        for pick, start, size in borrowed(w):
            n += dot(pick, in_n[start : start + size])
            c += dot(pick, in_g[start : start + size])
        nw[tp, w] = n.astype(bf16)
        gw[tp, w] = c.astype(bf16)
        for e in exchanges(w):
            e.start()

    def gather(w):
        for e in exchanges(w):
            e.wait_recv()
        rows = pl.ds(pl.multiple_of(w * SEQ, 16), SEQ)
        n = jnp.concatenate([nw[i, w].astype(f32)[:LEVEL] for i in (0, 1)])
        nf[rows, :] = n[:, :D].astype(bf16)
        gf[rows, :] = jnp.concatenate([gw[i, w].astype(f32)[:LEVEL] for i in (0, 1)]).astype(bf16)
        keys = jnp.concatenate([n[:, D:], n[:, D : D + SEQ - 128]], axis=1)
        t = lax.broadcasted_iota(jnp.int32, (SEQ, SEQ), 0)
        s = lax.broadcasted_iota(jnp.int32, (SEQ, SEQ), 1)
        region = lambda i: jnp.where(i >= LEVEL, i - LEVEL, i) >= LEVEL // 2
        last = ((w % 4) == 3).astype(jnp.int32) * lat
        crossing = jnp.where(region(t) != region(s), 1, 0) * last
        open_key = jnp.where(t == s, 1.0, keys)
        bias[w] = jnp.where((open_key == 1.0) & (crossing == 0), 0.0, -1e30)

    def project(p, w, count=1):
        rows, c = pl.ds(pl.multiple_of(w * SEQ, 16), count * SEQ), pl.ds(p * GROUP, GROUP)
        n = nf[rows, :]
        for j in range(3):
            o = dot(n, wq[j, :, c]).astype(bf16)
            qkv[j, rows, :] = o * bf16(0.125) if j == 0 else o
        da[rows, :] = dot(gf[rows, :], wo[c, :], NT).astype(bf16)

    lane = lax.broadcasted_iota(jnp.int32, (1, GROUP), 1) // 64
    heads = [(lane == h).astype(f32).astype(bf16) for h in range(HEADS)]

    def attend(p, w):
        rows, c = pl.ds(pl.multiple_of(w * SEQ, 16), SEQ), pl.ds(p * GROUP, GROUP)
        q, k, v, d = qkv[0, rows, :], qkv[1, rows, :], qkv[2, rows, :], da[rows, :]
        b = bias[w]
        v_t, k_t = v.T, k.T
        scores = dot(jnp.concatenate([k * m for m in heads]), q, NT)
        d_probs = dot(jnp.concatenate([v * m for m in heads]), d, NT)
        d_v, d_k = jnp.zeros((SEQ, GROUP), f32), jnp.zeros((SEQ, GROUP), f32)
        out_t, d_q_t = [], []
        for h in range(HEADS):
            s = scores[SEQ * h : SEQ * h + SEQ] + b
            e = jnp.exp(s - jnp.max(s, axis=0, keepdims=True))
            pr = e * (1.0 / jnp.sum(e, axis=0, keepdims=True))
            pb = pr.astype(bf16)
            u = pr * d_probs[SEQ * h : SEQ * h + SEQ]
            ds = (u - pr * jnp.sum(u, axis=0, keepdims=True)).astype(bf16)
            out_t.append(dot(v_t[64 * h : 64 * h + 64], pb))
            d_q_t.append(dot(k_t[64 * h : 64 * h + 64], ds))
            d_v += dot(pb, d * heads[h])
            d_k += dot(ds, q * heads[h])
        att[rows, c] = jnp.concatenate(out_t).astype(bf16).T
        dp[0, rows, c] = (jnp.concatenate(d_q_t) * 0.125).astype(bf16).T
        dp[1, rows, c] = d_k.astype(bf16)
        dp[2, rows, c] = d_v.astype(bf16)

    first, second = (y, px), (px, y)
    peers = ((along_y, along_x), (along_x, along_y))

    def halves(p, color, d):
        side = (1, 3).index(d)
        return copy(
            grads.at[p, color, (first[color] + 2) % 4, pl.ds(2 * side, 2)],
            half.at[p, color, side],
            half_s.at[p, color, side], half_r.at[p, color, side], peers[color][0][d - 1],
        )

    def stage(n, p, color, d):
        sems = (red_s.at[p, color, n, d - 1], red_r.at[p, color, n, d - 1])
        if n == 0:
            src = grads.at[p, color, (first[color] + d) % 4]
            return copy(src, got1.at[p, color, d // 2], *sems, peers[color][0][d - 1])
        if n == 1:
            src = mid1.at[p, color, (second[color] + d) % 4]
            return copy(src, got2.at[p, color, d - 1], *sems, peers[color][1][d - 1])
        src = mid2.at[p, color, ((z + d) % 4) // 2]
        return copy(src, got3.at[p, z, color], *sems, along_z[d - 1])

    def weight_grads(p):
        c = pl.ds(p * GROUP, GROUP)
        for d in (2, 1, 3, 0):
            row = (y + d) % 4
            a = n_t[pl.ds(pl.multiple_of(row * 256, 256), 256), :]
            col = (px + d) % 4
            pieces = [pl.ds(pl.multiple_of(i * 256 + col * 64, 64), 64) for i in range(4)]
            b = jnp.concatenate([n_t[i, :] for i in pieces])
            e = jnp.concatenate([g_t[i, :] for i in pieces])
            for color, m, val in (
                (0, 0, dot(a, dp[0, :, c])),
                (0, 1, dot(a, dp[1, :, c])),
                (1, 0, dot(b, dp[2, :, c])),
                (1, 1, dot(e, att[:, c])),
            ):
                val = val.astype(bf16)
                for i in range(4):
                    grads[p, color, (row, col)[color], i, m] = val[64 * i : 64 * i + 64]
            if d == 2:
                for color in (0, 1):
                    for side in (1, 3):
                        halves(p, color, side).start()

    def reduce_near(p):
        for color in (0, 1):
            for d in (1, 3):
                side = d // 2
                halves(p, color, d).wait_recv()
                to = (first[color] + d) % 4
                for i in range(2 * side, 2 * side + 2):
                    s = grads[p, color, to, i].astype(f32) + half[p, color, side, i - 2 * side].astype(f32)
                    grads[p, color, to, i] = s.astype(bf16)
                stage(0, p, color, d).start()

    def reduce_first(p):
        for color in (0, 1):
            for d in (1, 3):
                stage(0, p, color, d).wait_recv()

            @pl.loop(0, 4)
            def _(i):
                s = grads[p, color, first[color], i].astype(f32)
                for d in range(2):
                    s += got1[p, color, d, i].astype(f32)
                mid1[p, color, i] = s.astype(bf16)

            for d in (1, 2, 3):
                stage(1, p, color, d).start()

    def reduce_second(p):
        for color in (0, 1):
            for d in (1, 2, 3):
                stage(1, p, color, d).wait_recv()
            s = mid1[p, color, second[color]].astype(f32)
            for d in range(3):
                s += got2[p, color, d].astype(f32)
            s = s.astype(bf16)
            mid2[p, color, 0] = s[:, :32]
            mid2[p, color, 1] = s[:, 32:]
            got3[p, z, color] = mid2[p, color, z // 2]
            for d in (1, 2, 3):
                stage(2, p, color, d).start()

    def reduce_third(p):
        for color in (0, 1):
            for d in (1, 2, 3):
                stage(2, p, color, d).wait_recv()
            s = got3[p, 0, color].astype(f32)
            for i in range(1, 4):
                s += got3[p, i, color].astype(f32)
            for m in range(2):
                to = dwo if color and m else dwq.at[2 * color + m]
                to[:, p * GROUP : p * GROUP + GROUP] = s[m]

    def returned(w):
        return copy(back_out.at[w], total.at[w], back_s.at[w], back_r.at[w], other)

    def d_normed(first):
        rows = pl.ds(first * SEQ, 2 * SEQ)
        o = sum(dot(dp[j, rows, :], wq[j], NT) for j in range(3))
        pad = jnp.zeros((SLOT - LEVEL, D), f32)
        for w in (first, first + 1):
            v = o[(w - first) * SEQ : (w - first + 1) * SEQ]
            lo, hi = jnp.concatenate([v[:LEVEL], pad]), jnp.concatenate([v[LEVEL:], pad])
            mine[w] = jnp.where(tp == 0, lo, hi)
            back_out[w] = jnp.where(tp == 0, hi, lo).astype(bf16)
            returned(w).start()

    def add(w):
        returned(w).wait_recv()
        total[w] = (mine[w] + total[w].astype(f32)).astype(bf16)

    def transposed(i):
        rows = pl.ds(i * 128, 128)
        n_t[:, i * 128 : i * 128 + 128] = nf[rows, :].T
        g_t[:, i * 128 : i * 128 + 128] = gf[rows, :].T

    for w in range(EARLY - 1):
        assemble(w)
    pl.loop(0, EARLY - 1)(gather)
    for c in loads[5:]:
        c.wait()
    project(0, 0, 3)
    pl.loop(0, 3)(lambda w: attend(0, w))
    for c in halos[:2]:
        c.wait_recv()
    assemble(3)
    project(1, 0, 3)
    pl.loop(0, 3)(lambda w: attend(1, w))
    gather(jnp.int32(3))
    for p in range(PASSES):
        project(p, 3)
        attend(p, 3)
    for w in (0, 2):
        d_normed(w)
    for i in range(4):
        transposed(i)
    pl.loop(0, EARLY)(add)
    for c in halos[2:]:
        c.wait_recv()
    for w in range(EARLY, WINDOWS):
        assemble(w)

    @pl.loop(EARLY, WINDOWS)
    def _(w):
        gather(w)
        project(0, w)
        attend(0, w)

    for i in range(4, 9):
        transposed(i)
    weight_grads(0)
    project(1, EARLY, WINDOWS - EARLY)
    reduce_near(0)
    pl.loop(EARLY, WINDOWS)(lambda w: attend(1, w))
    weight_grads(1)
    for w in (4, 6):
        d_normed(w)
    reduce_first(0)
    reduce_near(1)
    pl.loop(EARLY, WINDOWS)(add)
    ret_out[:A_ROWS] = sum(dot(cols_t[b], total[4 + b]) for b in range(4)).astype(bf16)
    ret_out[A_ROWS:] = sum(dot(rest_t[j], total[3 + 4 * j]) for j in range(2)).astype(bf16)
    returns = []
    for i, peer in enumerate((from_a, to_b, from_c)):
        start, size = PARTS[i]
        rows = pl.ds(start, size)
        returns.append(copy(ret_out.at[rows], ret_in.at[rows], ret_s.at[i], ret_r.at[i], peer))
    for c in returns:
        c.start()
    local[:LEVEL] = jnp.zeros((LEVEL, D), f32)
    for b in range(4):
        o = dot(own_t[own_kind(b)], total[b]) + dot(own_t[own_kind(b + 4)], total[b + 4])
        skip = 72 + 144 * b - BAND_START[b]
        size = 144 if b < 3 else 72
        local[72 + 144 * b : 72 + 144 * b + size] = o[skip : skip + size]
    reduce_second(0)
    reduce_first(1)
    reduce_third(0)
    reduce_second(1)
    for c in returns:
        c.wait_recv()

    @pl.loop(0, 4)
    def _(i):
        rows = pl.ds(pl.multiple_of(i * 144, 16), 144)
        dn = local[rows, :] + dot(send_t[rows, :], ret_in[...])
        s = rstd[rows, :]
        xh = (x[rows, :].astype(f32) - mean[rows, :]) * s
        inner = dn - jnp.mean(dn, axis=-1, keepdims=True) - xh * jnp.mean(dn * xh, axis=-1, keepdims=True)
        dtok[rows, :] = (s * inner + g[rows, :].astype(f32)).astype(bf16)

    reduce_third(1)
    for c in halos + returns:
        c.wait_send()

    @pl.loop(0, WINDOWS)
    def _(w):
        for e in exchanges(w):
            e.wait_send()
        returned(w).wait_send()

    for p in range(PASSES):
        for color in (0, 1):
            for d in (1, 2, 3):
                if d != 2:
                    halves(p, color, d).wait_send()
                    stage(0, p, color, d).wait_send()
                stage(1, p, color, d).wait_send()
                stage(2, p, color, d).wait_send()


def body(tokens, land_mask, qkv_weight, out_weight, out_grad):
    mask = jnp.broadcast_to(land_mask.reshape(OWN, 1).astype(bf16), (OWN, 128))
    constants = [jnp.asarray(a) for a in selections()]
    operands = [tokens.reshape(OWN, D), out_grad.reshape(OWN, D), mask, qkv_weight, out_weight] + constants
    vmem, dma = pltpu.VMEM, pltpu.SemaphoreType.DMA
    tokens_all = WINDOWS * SEQ
    in_place = [a for i, a in enumerate(operands) if i != 2]
    d_tokens, d_qkv_weight, d_out_weight = pl.pallas_call(
        kernel,
        out_shape=(
            jax.ShapeDtypeStruct((OWN, D), bf16),
            jax.ShapeDtypeStruct((3, 32, 512), f32),
            jax.ShapeDtypeStruct((32, 512), f32),
        ),
        in_specs=[pl.BlockSpec(memory_space=pltpu.VMEM if i == 2 else pl.ANY) for i in range(len(operands))],
        out_specs=[pl.BlockSpec(memory_space=pltpu.VMEM)] * 3,
        scratch_shapes=[vmem(a.shape, bf16) for a in in_place]
        + [
            vmem((OWN, WIDE), bf16),
            vmem((OWN, 1), f32),
            vmem((OWN, 1), f32),
            vmem((HALO, WIDE), bf16),
            vmem((HALO, D), bf16),
            vmem((HALO, WIDE), bf16),
            vmem((HALO, D), bf16),
            vmem((2, WINDOWS, SLOT, WIDE), bf16),
            vmem((2, WINDOWS, SLOT, D), bf16),
            vmem((tokens_all, D), bf16),
            vmem((tokens_all, D), bf16),
            vmem((D, tokens_all), bf16),
            vmem((D, tokens_all), bf16),
            vmem((WINDOWS, SEQ, SEQ), f32),
            vmem((3, tokens_all, GROUP), bf16),
            vmem((tokens_all, GROUP), bf16),
            vmem((tokens_all, 512), bf16),
            vmem((3, tokens_all, 512), bf16),
            vmem((PASSES, 2, 4, 4, 2, 64, GROUP), bf16),
            vmem((PASSES, 2, 2, 2, 2, 64, GROUP), bf16),
            vmem((PASSES, 2, 2, 4, 2, 64, GROUP), bf16),
            vmem((PASSES, 2, 4, 2, 64, GROUP), bf16),
            vmem((PASSES, 2, 3, 2, 64, GROUP), bf16),
            vmem((PASSES, 2, 2, 2, 32, GROUP), bf16),
            vmem((PASSES, 4, 2, 2, 32, GROUP), bf16),
            vmem((WINDOWS, SLOT, D), f32),
            vmem((WINDOWS, SLOT, D), bf16),
            vmem((WINDOWS, SLOT, D), bf16),
            vmem((HALO, D), bf16),
            vmem((HALO, D), bf16),
            vmem((OWN, D), f32),
            dma((len(in_place),)),
            dma((2, 3)),
            dma((2, 3)),
            dma((2, WINDOWS)),
            dma((2, WINDOWS)),
            dma((3,)),
            dma((3,)),
            dma((WINDOWS,)),
            dma((WINDOWS,)),
            dma((PASSES, 2, 2)),
            dma((PASSES, 2, 2)),
            dma((PASSES, 2, 3, 3)),
            dma((PASSES, 2, 3, 3)),
        ],
        compiler_params=pltpu.CompilerParams(
            collective_id=0, has_side_effects=True, vmem_limit_bytes=63 * 1024 * 1024
        ),
        name="swin_backward",
    )(*operands)
    return d_tokens.reshape(ROWS, COLS, 1, D), d_qkv_weight, d_out_weight.T


def solution(mesh):
    in_specs = (
        P("lat", "lon", "tp", None),
        P("lat", "lon", "tp"),
        P(None, None, "tp"),
        P("tp", None),
        P("lat", "lon", "tp", None),
    )
    out_specs = (P("lat", "lon", "tp", None), P(None, "lon", "tp"), P("tp", "lon"))
    return jax.shard_map(body, mesh=mesh, in_specs=in_specs, out_specs=out_specs, check_vma=False)
```

```python
import jax
import jax.numpy as jnp
import numpy as np
from jax import lax
from jax.experimental import pallas as pl
from jax.experimental.pallas import tpu as pltpu
from jax.sharding import PartitionSpec as P

f32, bf16 = jnp.float32, jnp.bfloat16
MESH = pl.DeviceIdType.MESH
NN = (((1,), (0,)), ((), ()))
NT = (((1,), (1,)), ((), ()))

D = 1024
HEADS = 4
GROUP = HEADS * 64
PASSES = 2
ROWS = COLS = 24
OWN = ROWS * COLS
WINDOWS = 8
LEVEL = 72
SEQ = 2 * LEVEL
SLOT = 80
EARLY = 4
WIDE = D + 128
A_ROWS, B_ROWS, C_ROWS = 128, 64, 32
BC_ROWS = B_ROWS + C_ROWS
HALO = A_ROWS + BC_ROWS
PARTS = ((0, A_ROWS), (A_ROWS, B_ROWS), (A_ROWS + B_ROWS, C_ROWS))
BAND_START = (64, 208, 352, 416)


def selections():
    send = np.zeros((HALO, OWN), np.float32)
    own = np.zeros((WINDOWS, SLOT, 160), np.float32)
    cols = np.zeros((4, SLOT, A_ROWS), np.float32)
    rest = np.zeros((2, SLOT, BC_ROWS), np.float32)
    for r in range(ROWS):
        for c in range(COLS):
            if r >= 3 and c < 6:
                send[(r - 3) * 6 + c, r * COLS + c] = 1
            elif r < 3 and c >= 6:
                send[A_ROWS + r * 18 + c - 6, r * COLS + c] = 1
            elif r < 3:
                send[A_ROWS + B_ROWS + r * 6 + c, r * COLS + c] = 1
    for j in range(2):
        for b in range(4):
            for i in range(6):
                for c in range(12):
                    t, r, col = i * 12 + c, 6 * b + i, 12 * j + c
                    if r < 21 and col < 18:
                        own[j * 4 + b, t, (r + 3) * COLS + col + 6 - BAND_START[b]] = 1
                    elif r < 21:
                        cols[b, t, r * 6 + col - 18] = 1
                    elif col < 18:
                        rest[j, t, (r - 21) * 18 + col] = 1
                    else:
                        rest[j, t, B_ROWS + (r - 21) * 6 + col - 18] = 1
    own = own[[0, 3, 4, 7]]
    swap = lambda a: np.ascontiguousarray(np.swapaxes(a, -1, -2))
    row, col = np.zeros((OWN, ROWS), np.float32), np.zeros((OWN, COLS), np.float32)
    row[np.arange(OWN), np.arange(OWN) // COLS] = 1
    col[np.arange(OWN), np.arange(OWN) % COLS] = 1
    return [a.astype(jnp.bfloat16) for a in (row, col, send, swap(send), own, swap(own), cols, swap(cols), rest, swap(rest))]


def own_kind(w):
    return (0, 0, 0, 1, 2, 2, 2, 3)[w]


def dot(a, b, dims=NN):
    return lax.dot_general(a, b, dims, preferred_element_type=f32)


def place():
    lat, lon, tp = (lax.axis_index(a) for a in ("lat", "lon", "tp"))
    return lon // 8, (lon // 2) % 4, (lon % 2) * 2 + lat, tp


def device_at(y, x, z, tp):
    return (z % 2, (y * 4 + x) * 2 + z // 2, tp)


def kernel(
    x_h, g_h, mask, wq_h, wo_h, row_mh, col_mh, send_mh, send_th, own_mh, own_th, cols_mh, cols_th, rest_mh, rest_th,
    dtok, dwq, dwo,
    x, g, wq, wo, row_m, col_m, send_m, send_t, own_m, own_t, cols_m, cols_t, rest_m, rest_t,
    nat, mean, rstd, out_n, out_g, in_n, in_g, nw, gw, nf, gf, n_t, g_t, bias, qkv, da, att, dp,
    grads, half, got1, mid1, got2, mid2, got3,
    mine, back_out, total, ret_out, ret_in, local,
    load_s, halo_s, halo_r, core_s, core_r, ret_s, ret_r, back_s, back_r, half_s, half_r, red_s, red_r,
):
    y, px, z, tp = place()
    lat, lon = lax.axis_index("lat"), lax.axis_index("lon")
    other = (lat, lon, 1 - tp)
    before, after = (lon + 31) % 32, (lon + 1) % 32
    along_y = [device_at((y + d) % 4, px, z, tp) for d in (1, 2, 3)]
    along_x = [device_at(y, (px + d) % 4, z, tp) for d in (1, 2, 3)]
    along_z = [device_at(y, px, (z + d) % 4, tp) for d in (1, 2, 3)]
    to_a, to_b, to_c = (lat, before, tp), (1 - lat, lon, tp), (1 - lat, before, tp)
    from_a, from_c = (lat, after, tp), (1 - lat, after, tp)

    pairs = (
        (g_h, g), (send_mh, send_m), (x_h, x), (row_mh, row_m), (col_mh, col_m), (own_mh, own_m), (wq_h, wq), (wo_h, wo),
        (rest_mh, rest_m), (cols_mh, cols_m), (send_th, send_t), (own_th, own_t), (cols_th, cols_t), (rest_th, rest_t),
    )
    loads = [pltpu.make_async_copy(a, b, load_s.at[i]) for i, (a, b) in enumerate(pairs)]
    for c in loads:
        c.start()

    barrier = pltpu.get_barrier_semaphore()
    greeted = [other, to_a, to_c, from_a, from_c] + along_y + along_x + along_z
    for peer in greeted:
        pl.semaphore_signal(barrier, inc=1, device_id=peer, device_id_type=MESH)

    def copy(src, dst, s, r, peer):
        return pltpu.make_async_remote_copy(
            src_ref=src, dst_ref=dst, send_sem=s, recv_sem=r, device_id=peer, device_id_type=MESH
        )

    halos = [[], []]
    for i, peer in ((1, to_b), (0, to_a), (2, to_c)):
        start, size = PARTS[i]
        rows = pl.ds(start, size)
        halos[0].append(copy(out_g.at[rows], in_g.at[rows], halo_s.at[0, i], halo_r.at[0, i], peer))
        halos[1].append(copy(out_n.at[rows], in_n.at[rows], halo_s.at[1, i], halo_r.at[1, i], peer))
    for c in loads[:2]:
        c.wait()
    out_g[...] = dot(send_m[...], g[...]).astype(bf16)
    pl.semaphore_wait(barrier, len(greeted))
    for c in halos[0]:
        c.start()

    for c in loads[2:6]:
        c.wait()
    open_rows = jnp.concatenate([mask[r].astype(f32) for r in range(ROWS)]).astype(bf16)
    open_own = jnp.sum(dot(row_m[...], open_rows) * col_m[...].astype(f32), axis=-1, keepdims=True)
    nat[:, D:] = jnp.broadcast_to(open_own, (OWN, 128)).astype(bf16)

    @pl.loop(0, OWN // 64)
    def _(i):
        rows = pl.ds(pl.multiple_of(i * 64, 64), 64)
        v = x[rows, :].astype(f32)
        m = jnp.mean(v, axis=-1, keepdims=True)
        v = v - m
        s = lax.rsqrt(jnp.mean(v * v, axis=-1, keepdims=True) + 1e-05)
        mean[rows, :] = m
        rstd[rows, :] = s
        nat[rows, :D] = (v * s).astype(bf16)

    out_n[...] = dot(send_m[...], nat[...]).astype(bf16)
    halos[1][0].start()

    def exchanges(w):
        return (
            copy(nw.at[tp, w], nw.at[tp, w], core_s.at[0, w], core_r.at[0, w], other),
            copy(gw.at[tp, w], gw.at[tp, w], core_s.at[1, w], core_r.at[1, w], other),
        )

    def borrowed(w):
        if w == 3:
            return [(rest_m[0, :, :B_ROWS], A_ROWS, B_ROWS)]
        if w == 7:
            return [(cols_m[3], 0, A_ROWS), (rest_m[1], A_ROWS, BC_ROWS)]
        return [(cols_m[w - 4], 0, A_ROWS)] if w > 3 else []

    def assemble(w):
        rows = pl.ds(BAND_START[w % 4], 160)
        n, c = dot(own_m[own_kind(w)], nat[rows, :]), dot(own_m[own_kind(w)], g[rows, :])
        for pick, start, size in borrowed(w):
            n += dot(pick, in_n[start : start + size])
            c += dot(pick, in_g[start : start + size])
        nw[tp, w] = n.astype(bf16)
        gw[tp, w] = c.astype(bf16)
        for e in exchanges(w):
            e.start()

    def gather(w):
        for e in exchanges(w):
            e.wait_recv()
        rows = pl.ds(pl.multiple_of(w * SEQ, 16), SEQ)
        n = jnp.concatenate([nw[i, w].astype(f32)[:LEVEL] for i in (0, 1)])
        nf[rows, :] = n[:, :D].astype(bf16)
        gf[rows, :] = jnp.concatenate([gw[i, w].astype(f32)[:LEVEL] for i in (0, 1)]).astype(bf16)
        keys = jnp.concatenate([n[:, D:], n[:, D : D + SEQ - 128]], axis=1)
        t = lax.broadcasted_iota(jnp.int32, (SEQ, SEQ), 0)
        s = lax.broadcasted_iota(jnp.int32, (SEQ, SEQ), 1)
        region = lambda i: jnp.where(i >= LEVEL, i - LEVEL, i) >= LEVEL // 2
        last = ((w % 4) == 3).astype(jnp.int32) * lat
        crossing = jnp.where(region(t) != region(s), 1, 0) * last
        open_key = jnp.where(t == s, 1.0, keys)
        bias[w] = jnp.where((open_key == 1.0) & (crossing == 0), 0.0, -1e30)

    def project(p, w, count=1):
        rows, c = pl.ds(pl.multiple_of(w * SEQ, 16), count * SEQ), pl.ds(p * GROUP, GROUP)
        o = dot(nf[rows, :], jnp.concatenate([wq[j, :, c] for j in range(3)], axis=1)).astype(bf16)
        for j in range(3):
            part = o[:, j * GROUP : (j + 1) * GROUP]
            qkv[j, rows, :] = part * bf16(0.125) if j == 0 else part
        da[rows, :] = dot(gf[rows, :], wo[c, :], NT).astype(bf16)

    lane = lax.broadcasted_iota(jnp.int32, (1, GROUP), 1) // 64
    heads = [(lane == h).astype(f32).astype(bf16) for h in range(HEADS)]

    def attend(p, w):
        rows, c = pl.ds(pl.multiple_of(w * SEQ, 16), SEQ), pl.ds(p * GROUP, GROUP)
        q, k, v, d = qkv[0, rows, :], qkv[1, rows, :], qkv[2, rows, :], da[rows, :]
        b = bias[w]
        v_t, k_t = v.T, k.T
        scores = dot(jnp.concatenate([k * m for m in heads]), q, NT)
        d_probs = dot(jnp.concatenate([v * m for m in heads]), d, NT)
        d_v, d_k = jnp.zeros((SEQ, GROUP), f32), jnp.zeros((SEQ, GROUP), f32)
        out_t, d_q_t = [], []
        for h in range(HEADS):
            s = scores[SEQ * h : SEQ * h + SEQ] + b
            e = jnp.exp(s - jnp.max(s, axis=0, keepdims=True))
            pr = e * (1.0 / jnp.sum(e, axis=0, keepdims=True))
            pb = pr.astype(bf16)
            u = pr * d_probs[SEQ * h : SEQ * h + SEQ]
            ds = (u - pr * jnp.sum(u, axis=0, keepdims=True)).astype(bf16)
            out_t.append(dot(v_t[64 * h : 64 * h + 64], pb))
            d_q_t.append(dot(k_t[64 * h : 64 * h + 64], ds))
            d_v += dot(pb, d * heads[h])
            d_k += dot(ds, q * heads[h])
        att[rows, c] = jnp.concatenate(out_t).astype(bf16).T
        dp[0, rows, c] = (jnp.concatenate(d_q_t) * 0.125).astype(bf16).T
        dp[1, rows, c] = d_k.astype(bf16)
        dp[2, rows, c] = d_v.astype(bf16)

    first, second = (y, px), (px, y)
    peers = ((along_y, along_x), (along_x, along_y))

    def halves(p, color, d, m):
        side = (1, 3).index(d)
        return copy(
            grads.at[p, color, m, (first[color] + 2) % 4, pl.ds(2 * side, 2)],
            half.at[p, color, m, side],
            half_s.at[p, color, m, side], half_r.at[p, color, m, side], peers[color][0][d - 1],
        )

    def stage(n, p, color, d, m):
        sems = (red_s.at[p, color, m, n, d - 1], red_r.at[p, color, m, n, d - 1])
        if n == 0:
            src = grads.at[p, color, m, (first[color] + d) % 4]
            return copy(src, got1.at[p, color, m, d // 2], *sems, peers[color][0][d - 1])
        if n == 1:
            src = mid1.at[p, color, m, (second[color] + d) % 4]
            return copy(src, got2.at[p, color, m, d - 1], *sems, peers[color][1][d - 1])
        src = mid2.at[p, color, m, ((z + d) % 4) // 2]
        return copy(src, got3.at[p, z, color, m], *sems, along_z[d - 1])

    def weight_grads(p):
        c = pl.ds(p * GROUP, GROUP)
        for d in (2, 1, 3, 0):
            row = (y + d) % 4
            a = n_t[pl.ds(pl.multiple_of(row * 256, 256), 256), :]
            col = (px + d) % 4
            pieces = [pl.ds(pl.multiple_of(i * 256 + col * 64, 64), 64) for i in range(4)]
            b = jnp.concatenate([n_t[i, :] for i in pieces])
            e = jnp.concatenate([g_t[i, :] for i in pieces])
            near = dot(a, jnp.concatenate([dp[0, :, c], dp[1, :, c]], axis=1))
            for color, m, val in (
                (0, 0, near[:, :GROUP]),
                (0, 1, near[:, GROUP:]),
                (1, 0, dot(b, dp[2, :, c])),
                (1, 1, dot(e, att[:, c])),
            ):
                val = val.astype(bf16)
                for i in range(4):
                    grads[p, color, m, (row, col)[color], i] = val[64 * i : 64 * i + 64]
                if d == 2:
                    for side in (1, 3):
                        halves(p, color, side, m).start()

    both = [(color, m) for m in range(2) for color in range(2)]

    def reduce_near(p):
        for color, m in both:
            for d in (1, 3):
                side = d // 2
                halves(p, color, d, m).wait_recv()
                to, rows = (first[color] + d) % 4, pl.ds(2 * side, 2)
                s = grads[p, color, m, to, rows].astype(f32) + half[p, color, m, side].astype(f32)
                grads[p, color, m, to, rows] = s.astype(bf16)
                stage(0, p, color, d, m).start()

    def reduce_first(p):
        for color, m in both:
            for d in (1, 3):
                stage(0, p, color, d, m).wait_recv()
            s = grads[p, color, m, first[color]].astype(f32)
            for d in range(2):
                s += got1[p, color, m, d].astype(f32)
            mid1[p, color, m] = s.astype(bf16)
            for d in (1, 2, 3):
                stage(1, p, color, d, m).start()

    def reduce_second(p):
        for color, m in both:
            for d in (1, 2, 3):
                stage(1, p, color, d, m).wait_recv()
            s = mid1[p, color, m, second[color]].astype(f32)
            for d in range(3):
                s += got2[p, color, m, d].astype(f32)
            s = s.astype(bf16)
            mid2[p, color, m, 0] = s[:32]
            mid2[p, color, m, 1] = s[32:]
            got3[p, z, color, m] = mid2[p, color, m, z // 2]
            for d in (1, 2, 3):
                stage(2, p, color, d, m).start()

    def reduce_third(p):
        for color, m in both:
            for d in (1, 2, 3):
                stage(2, p, color, d, m).wait_recv()
            s = got3[p, 0, color, m].astype(f32)
            for i in range(1, 4):
                s += got3[p, i, color, m].astype(f32)
            to = dwo if color and m else dwq.at[2 * color + m]
            to[:, p * GROUP : p * GROUP + GROUP] = s

    def returned(w):
        return copy(back_out.at[w], total.at[w], back_s.at[w], back_r.at[w], other)

    def d_normed(first):
        rows = pl.ds(first * SEQ, 2 * SEQ)
        o = sum(dot(dp[j, rows, :], wq[j], NT) for j in range(3))
        pad = jnp.zeros((SLOT - LEVEL, D), f32)
        for w in (first, first + 1):
            v = o[(w - first) * SEQ : (w - first + 1) * SEQ]
            lo, hi = jnp.concatenate([v[:LEVEL], pad]), jnp.concatenate([v[LEVEL:], pad])
            mine[w] = jnp.where(tp == 0, lo, hi)
            back_out[w] = jnp.where(tp == 0, hi, lo).astype(bf16)
            returned(w).start()

    def add(w):
        returned(w).wait_recv()
        total[w] = (mine[w] + total[w].astype(f32)).astype(bf16)

    def transposed(i):
        rows = pl.ds(i * 128, 128)
        n_t[:, i * 128 : i * 128 + 128] = nf[rows, :].T
        g_t[:, i * 128 : i * 128 + 128] = gf[rows, :].T

    for w in range(EARLY - 1):
        assemble(w)
    pl.loop(0, EARLY - 1)(gather)
    for c in halos[1][1:]:
        c.start()
    for c in loads[6:]:
        c.wait()
    for p in range(PASSES):
        project(p, 0, EARLY - 1)
        pl.loop(0, EARLY - 1)(lambda w, p=p: attend(p, w))
    for c in halos[0][:1] + halos[1][:1]:
        c.wait_recv()
    assemble(3)
    d_normed(0)
    for i in range(3):
        transposed(i)
    gather(jnp.int32(3))
    for p in range(PASSES):
        project(p, 3)
        attend(p, 3)
    d_normed(2)
    transposed(3)
    pl.loop(0, EARLY)(add)
    for c in halos[0][1:] + halos[1][1:]:
        c.wait_recv()
    for w in range(EARLY, WINDOWS):
        assemble(w)

    @pl.loop(EARLY, WINDOWS)
    def _(w):
        gather(w)
        project(0, w)
        attend(0, w)

    for i in range(4, 9):
        transposed(i)
    weight_grads(0)
    for p in range(1, PASSES):
        project(p, EARLY, WINDOWS - EARLY)
        reduce_near(p - 1)
        if p > 1:
            reduce_first(p - 2)
        pl.loop(EARLY, WINDOWS)(lambda w, p=p: attend(p, w))
        if p > 2:
            reduce_second(p - 3)
        weight_grads(p)
    last = PASSES - 1
    d_normed(4)
    d_normed(6)
    reduce_near(last)
    reduce_first(last - 1)
    if last > 1:
        reduce_second(last - 2)
    pl.loop(EARLY, WINDOWS)(add)
    ret_out[:A_ROWS] = sum(dot(cols_t[b], total[4 + b]) for b in range(4)).astype(bf16)
    ret_out[A_ROWS:] = sum(dot(rest_t[j], total[3 + 4 * j]) for j in range(2)).astype(bf16)
    returns = []
    for i, peer in enumerate((from_a, to_b, from_c)):
        start, size = PARTS[i]
        rows = pl.ds(start, size)
        returns.append(copy(ret_out.at[rows], ret_in.at[rows], ret_s.at[i], ret_r.at[i], peer))
    for c in returns:
        c.start()
    local[:LEVEL] = jnp.zeros((LEVEL, D), f32)
    for b in range(4):
        o = dot(own_t[own_kind(b)], total[b]) + dot(own_t[own_kind(b + 4)], total[b + 4])
        skip = 72 + 144 * b - BAND_START[b]
        size = 144 if b < 3 else 72
        local[72 + 144 * b : 72 + 144 * b + size] = o[skip : skip + size]
    for p in range(last - 1):
        reduce_third(p)
    reduce_second(last - 1)
    reduce_first(last)
    for c in returns:
        c.wait_recv()

    @pl.loop(0, 4)
    def _(i):
        rows = pl.ds(pl.multiple_of(i * 144, 16), 144)
        dn = local[rows, :] + dot(send_t[rows, :], ret_in[...])
        s = rstd[rows, :]
        xh = (x[rows, :].astype(f32) - mean[rows, :]) * s
        inner = dn - jnp.mean(dn, axis=-1, keepdims=True) - xh * jnp.mean(dn * xh, axis=-1, keepdims=True)
        dtok[rows, :] = (s * inner + g[rows, :].astype(f32)).astype(bf16)

    reduce_third(last - 1)
    reduce_second(last)
    reduce_third(last)
    for c in halos[0] + halos[1] + returns:
        c.wait_send()

    @pl.loop(0, WINDOWS)
    def _(w):
        for e in exchanges(w):
            e.wait_send()
        returned(w).wait_send()

    for p in range(PASSES):
        for color, m in both:
            for d in (1, 2, 3):
                if d != 2:
                    halves(p, color, d, m).wait_send()
                    stage(0, p, color, d, m).wait_send()
                stage(1, p, color, d, m).wait_send()
                stage(2, p, color, d, m).wait_send()


def body(tokens, land_mask, qkv_weight, out_weight, out_grad):
    mask = land_mask.reshape(ROWS, 1, COLS)
    constants = [jnp.asarray(a) for a in selections()]
    operands = [tokens.reshape(OWN, D), out_grad.reshape(OWN, D), mask, qkv_weight, out_weight] + constants
    vmem, dma = pltpu.VMEM, pltpu.SemaphoreType.DMA
    tokens_all = WINDOWS * SEQ
    in_place = [a for i, a in enumerate(operands) if i != 2]
    d_tokens, d_qkv_weight, d_out_weight = pl.pallas_call(
        kernel,
        out_shape=(
            jax.ShapeDtypeStruct((OWN, D), bf16),
            jax.ShapeDtypeStruct((3, 32, 512), f32),
            jax.ShapeDtypeStruct((32, 512), f32),
        ),
        in_specs=[pl.BlockSpec(memory_space=pltpu.VMEM if i == 2 else pl.ANY) for i in range(len(operands))],
        out_specs=[pl.BlockSpec(memory_space=pltpu.VMEM)] * 3,
        scratch_shapes=[vmem(a.shape, bf16) for a in in_place]
        + [
            vmem((OWN, WIDE), bf16),
            vmem((OWN, 1), f32),
            vmem((OWN, 1), f32),
            vmem((HALO, WIDE), bf16),
            vmem((HALO, D), bf16),
            vmem((HALO, WIDE), bf16),
            vmem((HALO, D), bf16),
            vmem((2, WINDOWS, SLOT, WIDE), bf16),
            vmem((2, WINDOWS, SLOT, D), bf16),
            vmem((tokens_all, D), bf16),
            vmem((tokens_all, D), bf16),
            vmem((D, tokens_all), bf16),
            vmem((D, tokens_all), bf16),
            vmem((WINDOWS, SEQ, SEQ), f32),
            vmem((3, tokens_all, GROUP), bf16),
            vmem((tokens_all, GROUP), bf16),
            vmem((tokens_all, 512), bf16),
            vmem((3, tokens_all, 512), bf16),
            vmem((PASSES, 2, 2, 4, 4, 64, GROUP), bf16),
            vmem((PASSES, 2, 2, 2, 2, 64, GROUP), bf16),
            vmem((PASSES, 2, 2, 2, 4, 64, GROUP), bf16),
            vmem((PASSES, 2, 2, 4, 64, GROUP), bf16),
            vmem((PASSES, 2, 2, 3, 64, GROUP), bf16),
            vmem((PASSES, 2, 2, 2, 32, GROUP), bf16),
            vmem((PASSES, 4, 2, 2, 32, GROUP), bf16),
            vmem((WINDOWS, SLOT, D), f32),
            vmem((WINDOWS, SLOT, D), bf16),
            vmem((WINDOWS, SLOT, D), bf16),
            vmem((HALO, D), bf16),
            vmem((HALO, D), bf16),
            vmem((OWN, D), f32),
            dma((len(in_place),)),
            dma((2, 3)),
            dma((2, 3)),
            dma((2, WINDOWS)),
            dma((2, WINDOWS)),
            dma((3,)),
            dma((3,)),
            dma((WINDOWS,)),
            dma((WINDOWS,)),
            dma((PASSES, 2, 2, 2)),
            dma((PASSES, 2, 2, 2)),
            dma((PASSES, 2, 2, 3, 3)),
            dma((PASSES, 2, 2, 3, 3)),
        ],
        compiler_params=pltpu.CompilerParams(
            collective_id=0, has_side_effects=True, vmem_limit_bytes=63 * 1024 * 1024
        ),
        name="swin_backward",
    )(*operands)
    return d_tokens.reshape(ROWS, COLS, 1, D), d_qkv_weight, d_out_weight.T


def solution(mesh):
    in_specs = (
        P("lat", "lon", "tp", None),
        P("lat", "lon", "tp"),
        P(None, None, "tp"),
        P("tp", None),
        P("lat", "lon", "tp", None),
    )
    out_specs = (P("lat", "lon", "tp", None), P(None, "lon", "tp"), P("tp", "lon"))
    return jax.shard_map(body, mesh=mesh, in_specs=in_specs, out_specs=out_specs, check_vma=False)
```

```python
import jax
import jax.numpy as jnp
import numpy as np
from jax import lax
from jax.experimental import pallas as pl
from jax.experimental.pallas import tpu as pltpu
from jax.sharding import PartitionSpec as P

f32, bf16 = jnp.float32, jnp.bfloat16
MESH = pl.DeviceIdType.MESH
NN = (((1,), (0,)), ((), ()))
NT = (((1,), (1,)), ((), ()))

D = 1024
HEADS = 4
GROUP = HEADS * 64
PASSES = 2
ROWS = COLS = 24
OWN = ROWS * COLS
WINDOWS = 8
LEVEL = 72
SEQ = 2 * LEVEL
SLOT = 80
EARLY = 4
WIDE = D + 128
A_ROWS, B_ROWS, C_ROWS = 128, 64, 32
BC_ROWS = B_ROWS + C_ROWS
HALO = A_ROWS + BC_ROWS
PARTS = ((0, A_ROWS), (A_ROWS, B_ROWS), (A_ROWS + B_ROWS, C_ROWS))
BAND_START = (64, 208, 352, 416)


def selections():
    send = np.zeros((HALO, OWN), np.float32)
    own = np.zeros((WINDOWS, SLOT, 160), np.float32)
    cols = np.zeros((4, SLOT, A_ROWS), np.float32)
    rest = np.zeros((2, SLOT, BC_ROWS), np.float32)
    for r in range(ROWS):
        for c in range(COLS):
            if r >= 3 and c < 6:
                send[(r - 3) * 6 + c, r * COLS + c] = 1
            elif r < 3 and c >= 6:
                send[A_ROWS + r * 18 + c - 6, r * COLS + c] = 1
            elif r < 3:
                send[A_ROWS + B_ROWS + r * 6 + c, r * COLS + c] = 1
    for j in range(2):
        for b in range(4):
            for i in range(6):
                for c in range(12):
                    t, r, col = i * 12 + c, 6 * b + i, 12 * j + c
                    if r < 21 and col < 18:
                        own[j * 4 + b, t, (r + 3) * COLS + col + 6 - BAND_START[b]] = 1
                    elif r < 21:
                        cols[b, t, r * 6 + col - 18] = 1
                    elif col < 18:
                        rest[j, t, (r - 21) * 18 + col] = 1
                    else:
                        rest[j, t, B_ROWS + (r - 21) * 6 + col - 18] = 1
    own = own[[0, 3, 4, 7]]
    swap = lambda a: np.ascontiguousarray(np.swapaxes(a, -1, -2))
    row, col = np.zeros((OWN, ROWS), np.float32), np.zeros((OWN, COLS), np.float32)
    row[np.arange(OWN), np.arange(OWN) // COLS] = 1
    col[np.arange(OWN), np.arange(OWN) % COLS] = 1
    return [a.astype(jnp.bfloat16) for a in (row, col, send, swap(send), own, swap(own), cols, swap(cols), rest, swap(rest))]


def own_kind(w):
    return (0, 0, 0, 1, 2, 2, 2, 3)[w]


def dot(a, b, dims=NN):
    return lax.dot_general(a, b, dims, preferred_element_type=f32)


def place():
    lat, lon, tp = (lax.axis_index(a) for a in ("lat", "lon", "tp"))
    return lon // 8, (lon // 2) % 4, (lon % 2) * 2 + lat, tp


def device_at(y, x, z, tp):
    return (z % 2, (y * 4 + x) * 2 + z // 2, tp)


def kernel(
    x_h, g_h, mask, wq_h, wo_h, row_mh, col_mh, send_mh, send_th, own_mh, own_th, cols_mh, cols_th, rest_mh, rest_th,
    dtok, dwq, dwo,
    x, g, wq, wo, row_m, col_m, send_m, send_t, own_m, own_t, cols_m, cols_t, rest_m, rest_t,
    nat, mean, rstd, out_n, out_g, in_n, in_g, nw, gw, nf, gf, n_t, g_t, bias, qkv, da, att, dp,
    grads, half, got1, mid1, got2, mid2, got3,
    mine, back_out, total, ret_out, ret_in, local,
    load_s, halo_s, halo_r, core_s, core_r, ret_s, ret_r, back_s, back_r, half_s, half_r, red_s, red_r,
):
    y, px, z, tp = place()
    lat, lon = lax.axis_index("lat"), lax.axis_index("lon")
    other = (lat, lon, 1 - tp)
    before, after = (lon + 31) % 32, (lon + 1) % 32
    along_y = [device_at((y + d) % 4, px, z, tp) for d in (1, 2, 3)]
    along_x = [device_at(y, (px + d) % 4, z, tp) for d in (1, 2, 3)]
    along_z = [device_at(y, px, (z + d) % 4, tp) for d in (1, 2, 3)]
    to_a, to_b, to_c = (lat, before, tp), (1 - lat, lon, tp), (1 - lat, before, tp)
    from_a, from_c = (lat, after, tp), (1 - lat, after, tp)

    pairs = (
        (g_h, g), (send_mh, send_m), (x_h, x), (row_mh, row_m), (col_mh, col_m), (own_mh, own_m), (wq_h, wq), (wo_h, wo),
        (rest_mh, rest_m), (cols_mh, cols_m), (send_th, send_t), (own_th, own_t), (cols_th, cols_t), (rest_th, rest_t),
    )
    loads = [pltpu.make_async_copy(a, b, load_s.at[i]) for i, (a, b) in enumerate(pairs)]
    for c in loads:
        c.start()

    barrier = pltpu.get_barrier_semaphore()
    greeted = [other, to_a, to_c, from_a, from_c] + along_y + along_x + along_z
    for peer in greeted:
        pl.semaphore_signal(barrier, inc=1, device_id=peer, device_id_type=MESH)

    def copy(src, dst, s, r, peer):
        return pltpu.make_async_remote_copy(
            src_ref=src, dst_ref=dst, send_sem=s, recv_sem=r, device_id=peer, device_id_type=MESH
        )

    halos = [[], []]
    for i, peer in ((1, to_b), (0, to_a), (2, to_c)):
        start, size = PARTS[i]
        rows = pl.ds(start, size)
        halos[0].append(copy(out_g.at[rows], in_g.at[rows], halo_s.at[0, i], halo_r.at[0, i], peer))
        halos[1].append(copy(out_n.at[rows], in_n.at[rows], halo_s.at[1, i], halo_r.at[1, i], peer))
    for c in loads[:2]:
        c.wait()
    out_g[...] = dot(send_m[...], g[...]).astype(bf16)
    pl.semaphore_wait(barrier, len(greeted))
    halos[0][0].start()

    for c in loads[2:6]:
        c.wait()
    open_rows = jnp.concatenate([mask[r].astype(f32) for r in range(ROWS)]).astype(bf16)
    open_own = jnp.sum(dot(row_m[...], open_rows) * col_m[...].astype(f32), axis=-1, keepdims=True)
    nat[:, D:] = jnp.broadcast_to(open_own, (OWN, 128)).astype(bf16)

    @pl.loop(0, OWN // 64)
    def _(i):
        rows = pl.ds(pl.multiple_of(i * 64, 64), 64)
        v = x[rows, :].astype(f32)
        m = jnp.mean(v, axis=-1, keepdims=True)
        v = v - m
        s = lax.rsqrt(jnp.mean(v * v, axis=-1, keepdims=True) + 1e-05)
        mean[rows, :] = m
        rstd[rows, :] = s
        nat[rows, :D] = (v * s).astype(bf16)

    out_n[...] = dot(send_m[...], nat[...]).astype(bf16)
    halos[1][0].start()

    def exchanges(w):
        return (
            copy(nw.at[tp, w], nw.at[tp, w], core_s.at[0, w], core_r.at[0, w], other),
            copy(gw.at[tp, w], gw.at[tp, w], core_s.at[1, w], core_r.at[1, w], other),
        )

    def borrowed(w):
        if w == 3:
            return [(rest_m[0, :, :B_ROWS], A_ROWS, B_ROWS)]
        if w == 7:
            return [(cols_m[3], 0, A_ROWS), (rest_m[1], A_ROWS, BC_ROWS)]
        return [(cols_m[w - 4], 0, A_ROWS)] if w > 3 else []

    def assemble(w):
        rows = pl.ds(BAND_START[w % 4], 160)
        n, c = dot(own_m[own_kind(w)], nat[rows, :]), dot(own_m[own_kind(w)], g[rows, :])
        for pick, start, size in borrowed(w):
            n += dot(pick, in_n[start : start + size])
            c += dot(pick, in_g[start : start + size])
        nw[tp, w] = n.astype(bf16)
        gw[tp, w] = c.astype(bf16)
        for e in exchanges(w):
            e.start()

    def gather(w):
        for e in exchanges(w):
            e.wait_recv()
        rows = pl.ds(pl.multiple_of(w * SEQ, 16), SEQ)
        n = jnp.concatenate([nw[i, w].astype(f32)[:LEVEL] for i in (0, 1)])
        nf[rows, :] = n[:, :D].astype(bf16)
        gf[rows, :] = jnp.concatenate([gw[i, w].astype(f32)[:LEVEL] for i in (0, 1)]).astype(bf16)
        keys = jnp.concatenate([n[:, D:], n[:, D : D + SEQ - 128]], axis=1)
        t = lax.broadcasted_iota(jnp.int32, (SEQ, SEQ), 0)
        s = lax.broadcasted_iota(jnp.int32, (SEQ, SEQ), 1)
        region = lambda i: jnp.where(i >= LEVEL, i - LEVEL, i) >= LEVEL // 2
        last = ((w % 4) == 3).astype(jnp.int32) * lat
        crossing = jnp.where(region(t) != region(s), 1, 0) * last
        open_key = jnp.where(t == s, 1.0, keys)
        bias[w] = jnp.where((open_key == 1.0) & (crossing == 0), 0.0, -1e30)

    def project(p, w, count=1):
        rows, c = pl.ds(pl.multiple_of(w * SEQ, 16), count * SEQ), pl.ds(p * GROUP, GROUP)
        o = dot(nf[rows, :], jnp.concatenate([wq[j, :, c] for j in range(3)], axis=1)).astype(bf16)
        for j in range(3):
            part = o[:, j * GROUP : (j + 1) * GROUP]
            qkv[j, rows, :] = part * bf16(0.125) if j == 0 else part
        da[rows, :] = dot(gf[rows, :], wo[c, :], NT).astype(bf16)

    lane = lax.broadcasted_iota(jnp.int32, (1, GROUP), 1) // 64
    heads = [(lane == h).astype(f32).astype(bf16) for h in range(HEADS)]

    def attend(p, w):
        rows, c = pl.ds(pl.multiple_of(w * SEQ, 16), SEQ), pl.ds(p * GROUP, GROUP)
        q, k, v, d = qkv[0, rows, :], qkv[1, rows, :], qkv[2, rows, :], da[rows, :]
        b = bias[w]
        v_t, k_t = v.T, k.T
        scores = dot(jnp.concatenate([k * m for m in heads]), q, NT)
        d_probs = dot(jnp.concatenate([v * m for m in heads]), d, NT)
        d_v, d_k = jnp.zeros((SEQ, GROUP), f32), jnp.zeros((SEQ, GROUP), f32)
        out_t, d_q_t = [], []
        for h in range(HEADS):
            s = scores[SEQ * h : SEQ * h + SEQ] + b
            e = jnp.exp(s - jnp.max(s, axis=0, keepdims=True))
            pr = e * (1.0 / jnp.sum(e, axis=0, keepdims=True))
            pb = pr.astype(bf16)
            u = pr * d_probs[SEQ * h : SEQ * h + SEQ]
            ds = (u - pr * jnp.sum(u, axis=0, keepdims=True)).astype(bf16)
            out_t.append(dot(v_t[64 * h : 64 * h + 64], pb))
            d_q_t.append(dot(k_t[64 * h : 64 * h + 64], ds))
            d_v += dot(pb, d * heads[h])
            d_k += dot(ds, q * heads[h])
        att[rows, c] = jnp.concatenate(out_t).astype(bf16).T
        dp[0, rows, c] = (jnp.concatenate(d_q_t) * 0.125).astype(bf16).T
        dp[1, rows, c] = d_k.astype(bf16)
        dp[2, rows, c] = d_v.astype(bf16)

    first, second = (y, px), (px, y)
    peers = ((along_y, along_x), (along_x, along_y))

    def halves(p, color, d, m):
        side = (1, 3).index(d)
        return copy(
            grads.at[p, color, m, (first[color] + 2) % 4, pl.ds(2 * side, 2)],
            half.at[p, color, m, side],
            half_s.at[p, color, m, side], half_r.at[p, color, m, side], peers[color][0][d - 1],
        )

    def stage(n, p, color, d, m):
        sems = (red_s.at[p, color, m, n, d - 1], red_r.at[p, color, m, n, d - 1])
        if n == 0:
            src = grads.at[p, color, m, (first[color] + d) % 4]
            return copy(src, got1.at[p, color, m, d // 2], *sems, peers[color][0][d - 1])
        if n == 1:
            src = mid1.at[p, color, m, (second[color] + d) % 4]
            return copy(src, got2.at[p, color, m, d - 1], *sems, peers[color][1][d - 1])
        src = mid2.at[p, color, m, ((z + d) % 4) // 2]
        return copy(src, got3.at[p, z, color, m], *sems, along_z[d - 1])

    def weight_grads(p):
        c = pl.ds(p * GROUP, GROUP)
        for d in (2, 1, 3, 0):
            row = (y + d) % 4
            a = n_t[pl.ds(pl.multiple_of(row * 256, 256), 256), :]
            col = (px + d) % 4
            pieces = [pl.ds(pl.multiple_of(i * 256 + col * 64, 64), 64) for i in range(4)]
            b = jnp.concatenate([n_t[i, :] for i in pieces])
            e = jnp.concatenate([g_t[i, :] for i in pieces])
            near = dot(a, jnp.concatenate([dp[0, :, c], dp[1, :, c]], axis=1))
            for color, m, val in (
                (0, 0, near[:, :GROUP]),
                (0, 1, near[:, GROUP:]),
                (1, 0, dot(b, dp[2, :, c])),
                (1, 1, dot(e, att[:, c])),
            ):
                val = val.astype(bf16)
                for i in range(4):
                    grads[p, color, m, (row, col)[color], i] = val[64 * i : 64 * i + 64]
                if d == 2:
                    for side in (1, 3):
                        halves(p, color, side, m).start()

    both = [(color, m) for m in range(2) for color in range(2)]

    def reduce_near(p):
        for color, m in both:
            for d in (1, 3):
                side = d // 2
                halves(p, color, d, m).wait_recv()
                to, rows = (first[color] + d) % 4, pl.ds(2 * side, 2)
                s = grads[p, color, m, to, rows].astype(f32) + half[p, color, m, side].astype(f32)
                grads[p, color, m, to, rows] = s.astype(bf16)
                stage(0, p, color, d, m).start()

    def reduce_first(p):
        for color, m in both:
            for d in (1, 3):
                stage(0, p, color, d, m).wait_recv()
            s = grads[p, color, m, first[color]].astype(f32)
            for d in range(2):
                s += got1[p, color, m, d].astype(f32)
            mid1[p, color, m] = s.astype(bf16)
            for d in (1, 2, 3):
                stage(1, p, color, d, m).start()

    def reduce_second(p):
        for color, m in both:
            for d in (1, 2, 3):
                stage(1, p, color, d, m).wait_recv()
            s = mid1[p, color, m, second[color]].astype(f32)
            for d in range(3):
                s += got2[p, color, m, d].astype(f32)
            s = s.astype(bf16)
            mid2[p, color, m, 0] = s[:32]
            mid2[p, color, m, 1] = s[32:]
            got3[p, z, color, m] = mid2[p, color, m, z // 2]
            for d in (1, 2, 3):
                stage(2, p, color, d, m).start()

    def reduce_third(p):
        for color, m in both:
            for d in (1, 2, 3):
                stage(2, p, color, d, m).wait_recv()
            s = got3[p, 0, color, m].astype(f32)
            for i in range(1, 4):
                s += got3[p, i, color, m].astype(f32)
            to = dwo if color and m else dwq.at[2 * color + m]
            to[:, p * GROUP : p * GROUP + GROUP] = s

    def returned(w):
        return copy(back_out.at[w], total.at[w], back_s.at[w], back_r.at[w], other)

    def d_normed(first):
        rows = pl.ds(first * SEQ, 2 * SEQ)
        o = sum(dot(dp[j, rows, :], wq[j], NT) for j in range(3))
        pad = jnp.zeros((SLOT - LEVEL, D), f32)
        for w in (first, first + 1):
            v = o[(w - first) * SEQ : (w - first + 1) * SEQ]
            lo, hi = jnp.concatenate([v[:LEVEL], pad]), jnp.concatenate([v[LEVEL:], pad])
            mine[w] = jnp.where(tp == 0, lo, hi)
            back_out[w] = jnp.where(tp == 0, hi, lo).astype(bf16)
            returned(w).start()

    def add(w):
        returned(w).wait_recv()
        total[w] = (mine[w] + total[w].astype(f32)).astype(bf16)

    def transposed(i):
        rows = pl.ds(i * 128, 128)
        n_t[:, i * 128 : i * 128 + 128] = nf[rows, :].T
        g_t[:, i * 128 : i * 128 + 128] = gf[rows, :].T

    for w in range(EARLY - 1):
        assemble(w)
    pl.loop(0, EARLY - 1)(gather)
    for c in halos[0][1:] + halos[1][1:]:
        c.start()
    for c in loads[6:]:
        c.wait()
    for p in range(PASSES):
        project(p, 0, EARLY - 1)
        pl.loop(0, EARLY - 1)(lambda w, p=p: attend(p, w))
    d_normed(0)
    for c in halos[0][:1] + halos[1][:1]:
        c.wait_recv()
    assemble(3)
    for i in range(3):
        transposed(i)
    gather(jnp.int32(3))
    for p in range(PASSES):
        project(p, 3)
        attend(p, 3)
    d_normed(2)
    transposed(3)
    for c in halos[0][1:] + halos[1][1:]:
        c.wait_recv()
    for w in range(EARLY, WINDOWS):
        assemble(w)

    @pl.loop(EARLY, WINDOWS)
    def _(w):
        gather(w)
        project(0, w)
        attend(0, w)

    for i in range(4, 9):
        transposed(i)
    weight_grads(0)
    for p in range(1, PASSES):
        project(p, EARLY, WINDOWS - EARLY)
        reduce_near(p - 1)
        if p > 1:
            reduce_first(p - 2)
        pl.loop(EARLY, WINDOWS)(lambda w, p=p: attend(p, w))
        if p > 2:
            reduce_second(p - 3)
        weight_grads(p)
    last = PASSES - 1
    d_normed(4)
    d_normed(6)
    reduce_near(last)
    reduce_first(last - 1)
    if last > 1:
        reduce_second(last - 2)
    pl.loop(EARLY - 1, WINDOWS)(add)
    ret_out[:A_ROWS] = sum(dot(cols_t[b], total[4 + b]) for b in range(4)).astype(bf16)
    ret_out[A_ROWS:] = sum(dot(rest_t[j], total[3 + 4 * j]) for j in range(2)).astype(bf16)
    returns = []
    for i, peer in enumerate((from_a, to_b, from_c)):
        start, size = PARTS[i]
        rows = pl.ds(start, size)
        returns.append(copy(ret_out.at[rows], ret_in.at[rows], ret_s.at[i], ret_r.at[i], peer))
    for c in returns:
        c.start()
    pl.loop(0, EARLY - 1)(add)
    local[:LEVEL] = jnp.zeros((LEVEL, D), f32)
    for b in range(4):
        o = dot(own_t[own_kind(b)], total[b]) + dot(own_t[own_kind(b + 4)], total[b + 4])
        skip = 72 + 144 * b - BAND_START[b]
        size = 144 if b < 3 else 72
        local[72 + 144 * b : 72 + 144 * b + size] = o[skip : skip + size]
    for p in range(last - 1):
        reduce_third(p)
    reduce_second(last - 1)
    reduce_first(last)
    reduce_third(last - 1)
    reduce_second(last)
    for c in returns:
        c.wait_recv()

    @pl.loop(0, 4)
    def _(i):
        rows = pl.ds(pl.multiple_of(i * 144, 16), 144)
        dn = local[rows, :] + dot(send_t[rows, :], ret_in[...])
        s = rstd[rows, :]
        xh = (x[rows, :].astype(f32) - mean[rows, :]) * s
        inner = dn - jnp.mean(dn, axis=-1, keepdims=True) - xh * jnp.mean(dn * xh, axis=-1, keepdims=True)
        dtok[rows, :] = (s * inner + g[rows, :].astype(f32)).astype(bf16)

    reduce_third(last)
    for c in halos[0] + halos[1] + returns:
        c.wait_send()

    @pl.loop(0, WINDOWS)
    def _(w):
        for e in exchanges(w):
            e.wait_send()
        returned(w).wait_send()

    for p in range(PASSES):
        for color, m in both:
            for d in (1, 2, 3):
                if d != 2:
                    halves(p, color, d, m).wait_send()
                    stage(0, p, color, d, m).wait_send()
                stage(1, p, color, d, m).wait_send()
                stage(2, p, color, d, m).wait_send()


def body(tokens, land_mask, qkv_weight, out_weight, out_grad):
    mask = land_mask.reshape(ROWS, 1, COLS)
    constants = [jnp.asarray(a) for a in selections()]
    operands = [tokens.reshape(OWN, D), out_grad.reshape(OWN, D), mask, qkv_weight, out_weight] + constants
    vmem, dma = pltpu.VMEM, pltpu.SemaphoreType.DMA
    tokens_all = WINDOWS * SEQ
    in_place = [a for i, a in enumerate(operands) if i != 2]
    d_tokens, d_qkv_weight, d_out_weight = pl.pallas_call(
        kernel,
        out_shape=(
            jax.ShapeDtypeStruct((OWN, D), bf16),
            jax.ShapeDtypeStruct((3, 32, 512), f32),
            jax.ShapeDtypeStruct((32, 512), f32),
        ),
        in_specs=[pl.BlockSpec(memory_space=pltpu.VMEM if i == 2 else pl.ANY) for i in range(len(operands))],
        out_specs=[pl.BlockSpec(memory_space=pltpu.VMEM)] * 3,
        scratch_shapes=[vmem(a.shape, bf16) for a in in_place]
        + [
            vmem((OWN, WIDE), bf16),
            vmem((OWN, 1), f32),
            vmem((OWN, 1), f32),
            vmem((HALO, WIDE), bf16),
            vmem((HALO, D), bf16),
            vmem((HALO, WIDE), bf16),
            vmem((HALO, D), bf16),
            vmem((2, WINDOWS, SLOT, WIDE), bf16),
            vmem((2, WINDOWS, SLOT, D), bf16),
            vmem((tokens_all, D), bf16),
            vmem((tokens_all, D), bf16),
            vmem((D, tokens_all), bf16),
            vmem((D, tokens_all), bf16),
            vmem((WINDOWS, SEQ, SEQ), f32),
            vmem((3, tokens_all, GROUP), bf16),
            vmem((tokens_all, GROUP), bf16),
            vmem((tokens_all, 512), bf16),
            vmem((3, tokens_all, 512), bf16),
            vmem((PASSES, 2, 2, 4, 4, 64, GROUP), bf16),
            vmem((PASSES, 2, 2, 2, 2, 64, GROUP), bf16),
            vmem((PASSES, 2, 2, 2, 4, 64, GROUP), bf16),
            vmem((PASSES, 2, 2, 4, 64, GROUP), bf16),
            vmem((PASSES, 2, 2, 3, 64, GROUP), bf16),
            vmem((PASSES, 2, 2, 2, 32, GROUP), bf16),
            vmem((PASSES, 4, 2, 2, 32, GROUP), bf16),
            vmem((WINDOWS, SLOT, D), f32),
            vmem((WINDOWS, SLOT, D), bf16),
            vmem((WINDOWS, SLOT, D), bf16),
            vmem((HALO, D), bf16),
            vmem((HALO, D), bf16),
            vmem((OWN, D), f32),
            dma((len(in_place),)),
            dma((2, 3)),
            dma((2, 3)),
            dma((2, WINDOWS)),
            dma((2, WINDOWS)),
            dma((3,)),
            dma((3,)),
            dma((WINDOWS,)),
            dma((WINDOWS,)),
            dma((PASSES, 2, 2, 2)),
            dma((PASSES, 2, 2, 2)),
            dma((PASSES, 2, 2, 3, 3)),
            dma((PASSES, 2, 2, 3, 3)),
        ],
        compiler_params=pltpu.CompilerParams(
            collective_id=0, has_side_effects=True, vmem_limit_bytes=63 * 1024 * 1024
        ),
        name="swin_backward",
    )(*operands)
    return d_tokens.reshape(ROWS, COLS, 1, D), d_qkv_weight, d_out_weight.T


def solution(mesh):
    in_specs = (
        P("lat", "lon", "tp", None),
        P("lat", "lon", "tp"),
        P(None, None, "tp"),
        P("tp", None),
        P("lat", "lon", "tp", None),
    )
    out_specs = (P("lat", "lon", "tp", None), P(None, "lon", "tp"), P("tp", "lon"))
    return jax.shard_map(body, mesh=mesh, in_specs=in_specs, out_specs=out_specs, check_vma=False)
```

```python
import jax
import jax.numpy as jnp
import numpy as np
from jax import lax
from jax.experimental import pallas as pl
from jax.experimental.pallas import tpu as pltpu
from jax.sharding import PartitionSpec as P

f32, bf16 = jnp.float32, jnp.bfloat16
MESH = pl.DeviceIdType.MESH
NN = (((1,), (0,)), ((), ()))
NT = (((1,), (1,)), ((), ()))

D = 1024
HEADS = 4
GROUP = HEADS * 64
PASSES = 2
ROWS = COLS = 24
OWN = ROWS * COLS
WINDOWS = 8
LEVEL = 72
SEQ = 2 * LEVEL
SLOT = 80
EARLY = 4
WIDE = D + 128
A_ROWS, B_ROWS, C_ROWS = 128, 64, 32
BC_ROWS = B_ROWS + C_ROWS
HALO = A_ROWS + BC_ROWS
PARTS = ((0, A_ROWS), (A_ROWS, B_ROWS), (A_ROWS + B_ROWS, C_ROWS))
BAND_START = (64, 208, 352, 416)


def selections():
    send = np.zeros((HALO, OWN), np.float32)
    own = np.zeros((WINDOWS, SLOT, 160), np.float32)
    cols = np.zeros((4, SLOT, A_ROWS), np.float32)
    rest = np.zeros((2, SLOT, BC_ROWS), np.float32)
    for r in range(ROWS):
        for c in range(COLS):
            if r >= 3 and c < 6:
                send[(r - 3) * 6 + c, r * COLS + c] = 1
            elif r < 3 and c >= 6:
                send[A_ROWS + r * 18 + c - 6, r * COLS + c] = 1
            elif r < 3:
                send[A_ROWS + B_ROWS + r * 6 + c, r * COLS + c] = 1
    for j in range(2):
        for b in range(4):
            for i in range(6):
                for c in range(12):
                    t, r, col = i * 12 + c, 6 * b + i, 12 * j + c
                    if r < 21 and col < 18:
                        own[j * 4 + b, t, (r + 3) * COLS + col + 6 - BAND_START[b]] = 1
                    elif r < 21:
                        cols[b, t, r * 6 + col - 18] = 1
                    elif col < 18:
                        rest[j, t, (r - 21) * 18 + col] = 1
                    else:
                        rest[j, t, B_ROWS + (r - 21) * 6 + col - 18] = 1
    own = own[[0, 3, 4, 7]]
    swap = lambda a: np.ascontiguousarray(np.swapaxes(a, -1, -2))
    row, col = np.zeros((OWN, ROWS), np.float32), np.zeros((OWN, COLS), np.float32)
    row[np.arange(OWN), np.arange(OWN) // COLS] = 1
    col[np.arange(OWN), np.arange(OWN) % COLS] = 1
    return [a.astype(jnp.bfloat16) for a in (row, col, send, swap(send), own, swap(own), cols, swap(cols), rest, swap(rest))]


def own_kind(w):
    return (0, 0, 0, 1, 2, 2, 2, 3)[w]


def dot(a, b, dims=NN):
    return lax.dot_general(a, b, dims, preferred_element_type=f32)


def place():
    lat, lon, tp = (lax.axis_index(a) for a in ("lat", "lon", "tp"))
    return lon // 8, (lon // 2) % 4, (lon % 2) * 2 + lat, tp


def device_at(y, x, z, tp):
    return (z % 2, (y * 4 + x) * 2 + z // 2, tp)


def kernel(
    x_h, g_h, mask, wq_h, wo_h, row_mh, col_mh, send_mh, send_th, own_mh, own_th, cols_mh, cols_th, rest_mh, rest_th,
    dtok, dwq, dwo,
    x, g, wq, wo, row_m, col_m, send_m, send_t, own_m, own_t, cols_m, cols_t, rest_m, rest_t,
    nat, mean, rstd, out_n, out_g, in_n, in_g, nw, gw, nf, gf, n_t, g_t, bias, qkv, da, att, dp,
    grads, half, got1, mid1, got2, mid2, got3,
    mine, back_out, total, ret_out, ret_in, local,
    load_s, halo_s, halo_r, core_s, core_r, ret_s, ret_r, back_s, back_r, half_s, half_r, red_s, red_r,
):
    y, px, z, tp = place()
    lat, lon = lax.axis_index("lat"), lax.axis_index("lon")
    other = (lat, lon, 1 - tp)
    before, after = (lon + 31) % 32, (lon + 1) % 32
    along_y = [device_at((y + d) % 4, px, z, tp) for d in (1, 2, 3)]
    along_x = [device_at(y, (px + d) % 4, z, tp) for d in (1, 2, 3)]
    along_z = [device_at(y, px, (z + d) % 4, tp) for d in (1, 2, 3)]
    to_a, to_b, to_c = (lat, before, tp), (1 - lat, lon, tp), (1 - lat, before, tp)
    from_a, from_c = (lat, after, tp), (1 - lat, after, tp)

    pairs = (
        (g_h, g), (send_mh, send_m), (x_h, x), (row_mh, row_m), (col_mh, col_m), (own_mh, own_m), (wq_h, wq), (wo_h, wo),
        (rest_mh, rest_m), (cols_mh, cols_m), (send_th, send_t), (own_th, own_t), (cols_th, cols_t), (rest_th, rest_t),
    )
    loads = [pltpu.make_async_copy(a, b, load_s.at[i]) for i, (a, b) in enumerate(pairs)]
    for c in loads:
        c.start()

    barrier = pltpu.get_barrier_semaphore()
    greeted = [other, to_a, to_c, from_a, from_c] + along_y + along_x + along_z
    for peer in greeted:
        pl.semaphore_signal(barrier, inc=1, device_id=peer, device_id_type=MESH)

    def copy(src, dst, s, r, peer):
        return pltpu.make_async_remote_copy(
            src_ref=src, dst_ref=dst, send_sem=s, recv_sem=r, device_id=peer, device_id_type=MESH
        )

    halos = [[], []]
    for i, peer in ((1, to_b), (0, to_a), (2, to_c)):
        start, size = PARTS[i]
        rows = pl.ds(start, size)
        halos[0].append(copy(out_g.at[rows], in_g.at[rows], halo_s.at[0, i], halo_r.at[0, i], peer))
        halos[1].append(copy(out_n.at[rows], in_n.at[rows], halo_s.at[1, i], halo_r.at[1, i], peer))
    for c in loads[:2]:
        c.wait()
    out_g[...] = dot(send_m[...], g[...]).astype(bf16)
    pl.semaphore_wait(barrier, len(greeted))
    for c in halos[0]:
        c.start()

    for c in loads[2:6]:
        c.wait()
    open_rows = jnp.concatenate([mask[r].astype(f32) for r in range(ROWS)]).astype(bf16)
    open_own = jnp.sum(dot(row_m[...], open_rows) * col_m[...].astype(f32), axis=-1, keepdims=True)
    nat[:, D:] = jnp.broadcast_to(open_own, (OWN, 128)).astype(bf16)

    @pl.loop(0, OWN // 64)
    def _(i):
        rows = pl.ds(pl.multiple_of(i * 64, 64), 64)
        v = x[rows, :].astype(f32)
        m = jnp.mean(v, axis=-1, keepdims=True)
        v = v - m
        s = lax.rsqrt(jnp.mean(v * v, axis=-1, keepdims=True) + 1e-05)
        mean[rows, :] = m
        rstd[rows, :] = s
        nat[rows, :D] = (v * s).astype(bf16)

    out_n[...] = dot(send_m[...], nat[...]).astype(bf16)
    for c in halos[1]:
        c.start()

    def exchanges(w):
        return (
            copy(nw.at[tp, w], nw.at[tp, w], core_s.at[0, w], core_r.at[0, w], other),
            copy(gw.at[tp, w], gw.at[tp, w], core_s.at[1, w], core_r.at[1, w], other),
        )

    def borrowed(w):
        if w == 3:
            return [(rest_m[0, :, :B_ROWS], A_ROWS, B_ROWS)]
        if w == 7:
            return [(cols_m[3], 0, A_ROWS), (rest_m[1], A_ROWS, BC_ROWS)]
        return [(cols_m[w - 4], 0, A_ROWS)] if w > 3 else []

    def assemble(w):
        rows = pl.ds(BAND_START[w % 4], 160)
        n, c = dot(own_m[own_kind(w)], nat[rows, :]), dot(own_m[own_kind(w)], g[rows, :])
        for pick, start, size in borrowed(w):
            n += dot(pick, in_n[start : start + size])
            c += dot(pick, in_g[start : start + size])
        nw[tp, w] = n.astype(bf16)
        gw[tp, w] = c.astype(bf16)
        for e in exchanges(w):
            e.start()

    def gather(w):
        for e in exchanges(w):
            e.wait_recv()
        rows = pl.ds(pl.multiple_of(w * SEQ, 16), SEQ)
        n = jnp.concatenate([nw[i, w].astype(f32)[:LEVEL] for i in (0, 1)])
        nf[rows, :] = n[:, :D].astype(bf16)
        gf[rows, :] = jnp.concatenate([gw[i, w].astype(f32)[:LEVEL] for i in (0, 1)]).astype(bf16)
        keys = jnp.concatenate([n[:, D:], n[:, D : D + SEQ - 128]], axis=1)
        t = lax.broadcasted_iota(jnp.int32, (SEQ, SEQ), 0)
        s = lax.broadcasted_iota(jnp.int32, (SEQ, SEQ), 1)
        region = lambda i: jnp.where(i >= LEVEL, i - LEVEL, i) >= LEVEL // 2
        last = ((w % 4) == 3).astype(jnp.int32) * lat
        crossing = jnp.where(region(t) != region(s), 1, 0) * last
        open_key = jnp.where(t == s, 1.0, keys)
        bias[w] = jnp.where((open_key == 1.0) & (crossing == 0), 0.0, -1e30)

    def project(p, w, count=1):
        rows, c = pl.ds(pl.multiple_of(w * SEQ, 16), count * SEQ), pl.ds(p * GROUP, GROUP)
        o = dot(nf[rows, :], jnp.concatenate([wq[j, :, c] for j in range(3)], axis=1)).astype(bf16)
        for j in range(3):
            part = o[:, j * GROUP : (j + 1) * GROUP]
            qkv[j, rows, :] = part * bf16(0.125) if j == 0 else part
        da[rows, :] = dot(gf[rows, :], wo[c, :], NT).astype(bf16)

    lane = lax.broadcasted_iota(jnp.int32, (1, GROUP), 1) // 64
    heads = [(lane == h).astype(f32).astype(bf16) for h in range(HEADS)]

    def attend(p, w):
        rows, c = pl.ds(pl.multiple_of(w * SEQ, 16), SEQ), pl.ds(p * GROUP, GROUP)
        q, k, v, d = qkv[0, rows, :], qkv[1, rows, :], qkv[2, rows, :], da[rows, :]
        b = bias[w]
        v_t, k_t = v.T, k.T
        scores = dot(jnp.concatenate([k * m for m in heads]), q, NT)
        d_probs = dot(jnp.concatenate([v * m for m in heads]), d, NT)
        d_v, d_k = jnp.zeros((SEQ, GROUP), f32), jnp.zeros((SEQ, GROUP), f32)
        out_t, d_q_t = [], []
        for h in range(HEADS):
            s = scores[SEQ * h : SEQ * h + SEQ] + b
            e = jnp.exp(s - jnp.max(s, axis=0, keepdims=True))
            pr = e * (1.0 / jnp.sum(e, axis=0, keepdims=True))
            pb = pr.astype(bf16)
            u = pr * d_probs[SEQ * h : SEQ * h + SEQ]
            ds = (u - pr * jnp.sum(u, axis=0, keepdims=True)).astype(bf16)
            out_t.append(dot(v_t[64 * h : 64 * h + 64], pb))
            d_q_t.append(dot(k_t[64 * h : 64 * h + 64], ds))
            d_v += dot(pb, d * heads[h])
            d_k += dot(ds, q * heads[h])
        att[rows, c] = jnp.concatenate(out_t).astype(bf16).T
        dp[0, rows, c] = (jnp.concatenate(d_q_t) * 0.125).astype(bf16).T
        dp[1, rows, c] = d_k.astype(bf16)
        dp[2, rows, c] = d_v.astype(bf16)

    first, second = (y, px), (px, y)
    peers = ((along_y, along_x), (along_x, along_y))

    def halves(p, color, d, m):
        side = (1, 3).index(d)
        return copy(
            grads.at[p, color, m, (first[color] + 2) % 4, pl.ds(2 * side, 2)],
            half.at[p, color, m, side],
            half_s.at[p, color, m, side], half_r.at[p, color, m, side], peers[color][0][d - 1],
        )

    def stage(n, p, color, d, m):
        sems = (red_s.at[p, color, m, n, d - 1], red_r.at[p, color, m, n, d - 1])
        if n == 0:
            src = grads.at[p, color, m, (first[color] + d) % 4]
            return copy(src, got1.at[p, color, m, d // 2], *sems, peers[color][0][d - 1])
        if n == 1:
            src = mid1.at[p, color, m, (second[color] + d) % 4]
            return copy(src, got2.at[p, color, m, d - 1], *sems, peers[color][1][d - 1])
        src = mid2.at[p, color, m, ((z + d) % 4) // 2]
        return copy(src, got3.at[p, z, color, m], *sems, along_z[d - 1])

    def weight_grads(p):
        c = pl.ds(p * GROUP, GROUP)
        for d in (2, 1, 3, 0):
            row = (y + d) % 4
            a = n_t[pl.ds(pl.multiple_of(row * 256, 256), 256), :]
            col = (px + d) % 4
            pieces = [pl.ds(pl.multiple_of(i * 256 + col * 64, 64), 64) for i in range(4)]
            b = jnp.concatenate([n_t[i, :] for i in pieces])
            e = jnp.concatenate([g_t[i, :] for i in pieces])
            near = dot(a, jnp.concatenate([dp[0, :, c], dp[1, :, c]], axis=1))
            for color, m, val in (
                (0, 0, near[:, :GROUP]),
                (0, 1, near[:, GROUP:]),
                (1, 0, dot(b, dp[2, :, c])),
                (1, 1, dot(e, att[:, c])),
            ):
                val = val.astype(bf16)
                for i in range(4):
                    grads[p, color, m, (row, col)[color], i] = val[64 * i : 64 * i + 64]
                if d == 2:
                    for side in (1, 3):
                        halves(p, color, side, m).start()

    both = [(color, m) for m in range(2) for color in range(2)]

    def reduce_near(p):
        for color, m in both:
            for d in (1, 3):
                side = d // 2
                halves(p, color, d, m).wait_recv()
                to, rows = (first[color] + d) % 4, pl.ds(2 * side, 2)
                s = grads[p, color, m, to, rows].astype(f32) + half[p, color, m, side].astype(f32)
                grads[p, color, m, to, rows] = s.astype(bf16)
                stage(0, p, color, d, m).start()

    def reduce_first(p):
        for color, m in both:
            for d in (1, 3):
                stage(0, p, color, d, m).wait_recv()
            s = grads[p, color, m, first[color]].astype(f32)
            for d in range(2):
                s += got1[p, color, m, d].astype(f32)
            mid1[p, color, m] = s.astype(bf16)
            for d in (1, 2, 3):
                stage(1, p, color, d, m).start()

    def reduce_second(p):
        for color, m in both:
            for d in (1, 2, 3):
                stage(1, p, color, d, m).wait_recv()
            s = mid1[p, color, m, second[color]].astype(f32)
            for d in range(3):
                s += got2[p, color, m, d].astype(f32)
            s = s.astype(bf16)
            mid2[p, color, m, 0] = s[:32]
            mid2[p, color, m, 1] = s[32:]
            got3[p, z, color, m] = mid2[p, color, m, z // 2]
            for d in (1, 2, 3):
                stage(2, p, color, d, m).start()

    def reduce_third(p):
        for color, m in both:
            for d in (1, 2, 3):
                stage(2, p, color, d, m).wait_recv()
            s = got3[p, 0, color, m].astype(f32)
            for i in range(1, 4):
                s += got3[p, i, color, m].astype(f32)
            to = dwo if color and m else dwq.at[2 * color + m]
            to[:, p * GROUP : p * GROUP + GROUP] = s

    def returned(w):
        return copy(back_out.at[w], total.at[w], back_s.at[w], back_r.at[w], other)

    def d_normed(first):
        rows = pl.ds(first * SEQ, 2 * SEQ)
        o = sum(dot(dp[j, rows, :], wq[j], NT) for j in range(3))
        pad = jnp.zeros((SLOT - LEVEL, D), f32)
        for w in (first, first + 1):
            v = o[(w - first) * SEQ : (w - first + 1) * SEQ]
            lo, hi = jnp.concatenate([v[:LEVEL], pad]), jnp.concatenate([v[LEVEL:], pad])
            mine[w] = jnp.where(tp == 0, lo, hi)
            back_out[w] = jnp.where(tp == 0, hi, lo).astype(bf16)
            returned(w).start()

    def add(w):
        returned(w).wait_recv()
        total[w] = (mine[w] + total[w].astype(f32)).astype(bf16)

    def transposed(i):
        rows = pl.ds(i * 128, 128)
        n_t[:, i * 128 : i * 128 + 128] = nf[rows, :].T
        g_t[:, i * 128 : i * 128 + 128] = gf[rows, :].T

    for w in range(EARLY - 1):
        assemble(w)
    pl.loop(0, EARLY - 1)(gather)
    for c in loads[6:]:
        c.wait()
    for p in range(PASSES):
        project(p, 0, EARLY - 1)
        pl.loop(0, EARLY - 1)(lambda w, p=p: attend(p, w))
    d_normed(0)
    for i in range(3):
        transposed(i)
    for c in halos[0][:1] + halos[1][:1]:
        c.wait_recv()
    assemble(3)
    gather(jnp.int32(3))
    for p in range(PASSES):
        project(p, 3)
        attend(p, 3)
    for c in halos[0][1:] + halos[1][1:]:
        c.wait_recv()
    for w in range(EARLY, WINDOWS):
        assemble(w)
    d_normed(2)
    transposed(3)

    @pl.loop(EARLY, WINDOWS)
    def _(w):
        gather(w)
        project(0, w)
        attend(0, w)

    for i in range(4, 9):
        transposed(i)
    weight_grads(0)
    for p in range(1, PASSES):
        project(p, EARLY, WINDOWS - EARLY)
        reduce_near(p - 1)
        if p > 1:
            reduce_first(p - 2)
        pl.loop(EARLY, WINDOWS)(lambda w, p=p: attend(p, w))
        if p > 2:
            reduce_second(p - 3)
        weight_grads(p)
    last = PASSES - 1
    d_normed(4)
    d_normed(6)
    reduce_near(last)
    reduce_first(last - 1)
    if last > 1:
        reduce_second(last - 2)
    pl.loop(EARLY - 1, WINDOWS)(add)
    ret_out[:A_ROWS] = sum(dot(cols_t[b], total[4 + b]) for b in range(4)).astype(bf16)
    ret_out[A_ROWS:] = sum(dot(rest_t[j], total[3 + 4 * j]) for j in range(2)).astype(bf16)
    returns = []
    for i, peer in enumerate((from_a, to_b, from_c)):
        start, size = PARTS[i]
        rows = pl.ds(start, size)
        returns.append(copy(ret_out.at[rows], ret_in.at[rows], ret_s.at[i], ret_r.at[i], peer))
    for c in returns:
        c.start()
    pl.loop(0, EARLY - 1)(add)
    local[:LEVEL] = jnp.zeros((LEVEL, D), f32)
    for b in range(4):
        o = dot(own_t[own_kind(b)], total[b]) + dot(own_t[own_kind(b + 4)], total[b + 4])
        skip = 72 + 144 * b - BAND_START[b]
        size = 144 if b < 3 else 72
        local[72 + 144 * b : 72 + 144 * b + size] = o[skip : skip + size]
    for p in range(last - 1):
        reduce_third(p)
    reduce_second(last - 1)
    reduce_first(last)
    reduce_third(last - 1)
    reduce_second(last)
    for c in returns:
        c.wait_recv()

    @pl.loop(0, 4)
    def _(i):
        rows = pl.ds(pl.multiple_of(i * 144, 16), 144)
        dn = local[rows, :] + dot(send_t[rows, :], ret_in[...])
        s = rstd[rows, :]
        xh = (x[rows, :].astype(f32) - mean[rows, :]) * s
        inner = dn - jnp.mean(dn, axis=-1, keepdims=True) - xh * jnp.mean(dn * xh, axis=-1, keepdims=True)
        dtok[rows, :] = (s * inner + g[rows, :].astype(f32)).astype(bf16)

    reduce_third(last)
    for c in halos[0] + halos[1] + returns:
        c.wait_send()

    @pl.loop(0, WINDOWS)
    def _(w):
        for e in exchanges(w):
            e.wait_send()
        returned(w).wait_send()

    for p in range(PASSES):
        for color, m in both:
            for d in (1, 2, 3):
                if d != 2:
                    halves(p, color, d, m).wait_send()
                    stage(0, p, color, d, m).wait_send()
                stage(1, p, color, d, m).wait_send()
                stage(2, p, color, d, m).wait_send()


def body(tokens, land_mask, qkv_weight, out_weight, out_grad):
    mask = land_mask.reshape(ROWS, 1, COLS)
    constants = [jnp.asarray(a) for a in selections()]
    operands = [tokens.reshape(OWN, D), out_grad.reshape(OWN, D), mask, qkv_weight, out_weight] + constants
    vmem, dma = pltpu.VMEM, pltpu.SemaphoreType.DMA
    tokens_all = WINDOWS * SEQ
    in_place = [a for i, a in enumerate(operands) if i != 2]
    d_tokens, d_qkv_weight, d_out_weight = pl.pallas_call(
        kernel,
        out_shape=(
            jax.ShapeDtypeStruct((OWN, D), bf16),
            jax.ShapeDtypeStruct((3, 32, 512), f32),
            jax.ShapeDtypeStruct((32, 512), f32),
        ),
        in_specs=[pl.BlockSpec(memory_space=pltpu.VMEM if i == 2 else pl.ANY) for i in range(len(operands))],
        out_specs=[pl.BlockSpec(memory_space=pltpu.VMEM)] * 3,
        scratch_shapes=[vmem(a.shape, bf16) for a in in_place]
        + [
            vmem((OWN, WIDE), bf16),
            vmem((OWN, 1), f32),
            vmem((OWN, 1), f32),
            vmem((HALO, WIDE), bf16),
            vmem((HALO, D), bf16),
            vmem((HALO, WIDE), bf16),
            vmem((HALO, D), bf16),
            vmem((2, WINDOWS, SLOT, WIDE), bf16),
            vmem((2, WINDOWS, SLOT, D), bf16),
            vmem((tokens_all, D), bf16),
            vmem((tokens_all, D), bf16),
            vmem((D, tokens_all), bf16),
            vmem((D, tokens_all), bf16),
            vmem((WINDOWS, SEQ, SEQ), f32),
            vmem((3, tokens_all, GROUP), bf16),
            vmem((tokens_all, GROUP), bf16),
            vmem((tokens_all, 512), bf16),
            vmem((3, tokens_all, 512), bf16),
            vmem((PASSES, 2, 2, 4, 4, 64, GROUP), bf16),
            vmem((PASSES, 2, 2, 2, 2, 64, GROUP), bf16),
            vmem((PASSES, 2, 2, 2, 4, 64, GROUP), bf16),
            vmem((PASSES, 2, 2, 4, 64, GROUP), bf16),
            vmem((PASSES, 2, 2, 3, 64, GROUP), bf16),
            vmem((PASSES, 2, 2, 2, 32, GROUP), bf16),
            vmem((PASSES, 4, 2, 2, 32, GROUP), bf16),
            vmem((WINDOWS, SLOT, D), f32),
            vmem((WINDOWS, SLOT, D), bf16),
            vmem((WINDOWS, SLOT, D), bf16),
            vmem((HALO, D), bf16),
            vmem((HALO, D), bf16),
            vmem((OWN, D), f32),
            dma((len(in_place),)),
            dma((2, 3)),
            dma((2, 3)),
            dma((2, WINDOWS)),
            dma((2, WINDOWS)),
            dma((3,)),
            dma((3,)),
            dma((WINDOWS,)),
            dma((WINDOWS,)),
            dma((PASSES, 2, 2, 2)),
            dma((PASSES, 2, 2, 2)),
            dma((PASSES, 2, 2, 3, 3)),
            dma((PASSES, 2, 2, 3, 3)),
        ],
        compiler_params=pltpu.CompilerParams(
            collective_id=0, has_side_effects=True, vmem_limit_bytes=63 * 1024 * 1024
        ),
        name="swin_backward",
    )(*operands)
    return d_tokens.reshape(ROWS, COLS, 1, D), d_qkv_weight, d_out_weight.T


def solution(mesh):
    in_specs = (
        P("lat", "lon", "tp", None),
        P("lat", "lon", "tp"),
        P(None, None, "tp"),
        P("tp", None),
        P("lat", "lon", "tp", None),
    )
    out_specs = (P("lat", "lon", "tp", None), P(None, "lon", "tp"), P("tp", "lon"))
    return jax.shard_map(body, mesh=mesh, in_specs=in_specs, out_specs=out_specs, check_vma=False)
```
